32 devices in a mesh: row: 8 (over y, x, core), col: 4 (over z).
Axes of the slice: x: 2, y: 2, z: 4, core: 2. Of those that a mesh axis runs over, the one named last changes fastest.
Arguments:
- sketch: bfloat16 [32, 64, 4, 3, 128], P('row', 'col'), may hold values from -6 to 6
- snapshots: bfloat16 [32, 64, 4, 3, 512], P('row', 'col'), may hold values from -6 to 6
- start_block: float32 [128, 64], replicated, may hold values from -0.5 to 0.5
Outputs:
- galerkin: float32 [64, 4096], replicated
The draws below stay inside these ranges and needn't reach their ends.
All inputs are finite; a program needn't handle non-finite values.
Results may differ from the reference program's by a relative error of at most 0.0084.
Values may be sent and summed in bfloat16 or wider, within the bound.
A program may use at most 64 MiB of HBM per device.

```python
import math
import jax
import jax.numpy as jnp
from jax import lax

NZ = 4
SNAP = 512
R = 128
M = 64
ITERS = 4
NX = 32
NY = 64


def block_levels(rng, extent, pieces, smallest, largest):
    factor_of, own = 1.0, jax.random.fold_in(rng, 6)
    for position, blocks in pieces:
        steps = jnp.exp(jax.random.uniform(jax.random.fold_in(own, position), (blocks,), jnp.float32, smallest / len(pieces), largest / len(pieces)))
        factor_of = factor_of * jnp.repeat(steps, extent[position] // blocks).reshape([-1 if axis == position else 1 for axis in range(len(extent))])
    return factor_of


def noise(own_key, extent, spread, most, split=(), kind=jnp.bfloat16):
    entries = spread * jax.random.normal(own_key, extent, jnp.float32)
    if split:
        entries = entries * block_levels(own_key, extent, split, -0.22, 0.18)
    return jnp.clip(entries, -most, most).astype(kind)


def setup_inputs(seed: int = 0) -> dict:
    arg_keys = jax.random.split(jax.random.key(seed), 4)
    sketch = noise(arg_keys[0], (NX, NY, NZ, 3, R), 1.0, 6.0, ((0, 8), (1, 4)))
    snapshots = noise(arg_keys[1], (NX, NY, NZ, 3, SNAP), 1.0, 6.0, ((0, 8), (1, 4)))
    start_block = noise(arg_keys[2], (R, M), R ** -0.5, 0.5, (), jnp.float32)
    return dict(sketch=sketch, snapshots=snapshots, start_block=start_block)


def reference(sketch, snapshots, start_block):
    highest = lax.Precision.HIGHEST
    flat_sketch = sketch.reshape(NX * NY * NZ * 3, R)
    flat_snap = snapshots.reshape(NX * NY * NZ * 3, SNAP)
    coeffs = lax.dot_general(flat_sketch, flat_snap, (((0,), (0,)), ((), ())), preferred_element_type=jnp.float32)
    projected = jnp.dot(coeffs.T, start_block, precision=highest)
    y_matrix = jnp.dot(coeffs, projected, precision=highest)
    polar = y_matrix / jnp.sqrt(jnp.sum(y_matrix * y_matrix) + 1e-06)
    for repeat in range(ITERS):
        polar = 1.5 * polar - 0.5 * jnp.dot(polar, jnp.dot(polar.T, polar, precision=highest), precision=highest)
    basis_bf = polar.astype(jnp.bfloat16)
    mode_values = jnp.dot(flat_sketch, basis_bf, preferred_element_type=jnp.float32).astype(jnp.bfloat16)
    mode_field = mode_values.reshape(NX, NY, NZ, 3, M)
    wide_field = mode_field.astype(jnp.float32)
    gradients = jnp.stack([(jnp.roll(wide_field, -1, axis=ax_num) - jnp.roll(wide_field, 1, axis=ax_num)) * 0.5 for ax_num in range(3)]).astype(jnp.bfloat16)

    def plane_step(total, plane_at):
        phi_plane = lax.dynamic_index_in_dim(mode_field, plane_at, 0, keepdims=False)
        grad_plane = lax.dynamic_index_in_dim(gradients, plane_at, 1, keepdims=False)
        advect = jnp.einsum('yzdi,dyzcj->yzcij', phi_plane.astype(jnp.float32), grad_plane.astype(jnp.float32)).astype(jnp.bfloat16)
        partial_term = lax.dot_general(phi_plane.reshape(NY * NZ * 3, M), advect.reshape(NY * NZ * 3, M * M), (((0,), (0,)), ((), ())), preferred_element_type=jnp.float32)
        return (total + partial_term, None)
    total, unused = lax.scan(plane_step, jnp.zeros((M, M * M), jnp.float32), jnp.arange(NX, dtype=jnp.int32))
    return total * (1.0 / math.sqrt(NX * NY * NZ))
```

```python
import functools
import math

import jax
import jax.numpy as jnp
import numpy as np
from jax import lax
from jax.experimental import pallas as pl
from jax.experimental.pallas import tpu as pltpu
from jax.sharding import PartitionSpec as P

ITERS = 4
MESH = pl.DeviceIdType.MESH
F32 = jnp.float32
BF16 = jnp.bfloat16
HIGHEST = lax.Precision.HIGHEST
NT = (((1,), (1,)), ((), ()))


def neighbour_columns(nx, ny, nz):
    plane = ny * nz
    cells = nx * plane
    slab = 16
    x, y, z = np.meshgrid(np.arange(nx), np.arange(ny), np.arange(nz), indexing="ij")
    cell = x * plane + y * nz + z
    x_before, x_after = cells, cells + plane
    y_before = cells + 2 * plane
    y_after = y_before + nx * slab
    ahead = [
        np.where(x < nx - 1, cell + plane, x_after + y * nz + z),
        np.where(y < ny - 1, cell + nz, y_after + x * slab + z),
        np.where(z < nz - 1, cell + 1, cell - (nz - 1)),
    ]
    behind = [
        np.where(x > 0, cell - plane, x_before + y * nz + z),
        np.where(y > 0, cell - nz, y_before + x * slab + slab - nz + z),
        np.where(z > 0, cell - 1, cell + nz - 1),
    ]
    both = [np.concatenate([v.reshape(-1) for v in side]) for side in (ahead, behind)]
    return np.stack(both).astype(np.int32)


def kernel(
    chips, cols, scale,
    c_ref, sk_ref, start_ref, near_ref, out_ref,
    hx, hy, rc1, acc1, rc2, rc3, cfull,
    diff, phi, phi_all, grad, adv,
    sg1, rg1, sg2, rg2, sg3, rg3, gfull,
    hs, hr, a1s, a1r, a2s, a2r, a3s, a3r, a4s, a4r, a5s, a5r,
    g1s, g1r, g2s, g2r, g3s, g3r, g4s, g4r, g5s, g5r, g6s, g6r,
):
    rows = 2 * chips
    row, col = lax.axis_index("row"), lax.axis_index("col")
    chip, core = row // 2, lax.rem(row, 2)
    sibling = (row + 1 - 2 * core, col)
    row_up, row_down = lax.rem(row + 1, rows), lax.rem(row + rows - 1, rows)
    col_up, col_down = lax.rem(col + 1, cols), lax.rem(col + cols - 1, cols)
    row_other = lax.rem(row + rows + 2 * core - 1, rows)

    def chip_at(offset):
        return lax.rem(chip + offset, chips)

    def col_at(offset):
        return lax.rem(col + offset, cols)

    def on_chip(q):
        return (2 * q + core, col)

    def push(src, dst, send, recv, device):
        return pltpu.make_async_remote_copy(
            src_ref=src, dst_ref=dst, send_sem=send, recv_sem=recv,
            device_id=device, device_id_type=MESH,
        )

    barrier = pltpu.get_barrier_semaphore()
    partners = [sibling, (row_other, col)]
    partners += [on_chip(chip_at(o)) for o in range(1, chips)]
    partners += [(row, col_at(o)) for o in range(1, cols)]
    for device in partners:
        pl.semaphore_signal(barrier, inc=1, device_id=device, device_id_type=MESH)
    pl.semaphore_wait(barrier, len(partners))

    a1 = push(c_ref.at[1 - core], rc1, a1s.at[0], a1r.at[0], sibling)
    a1.start()
    nx, plane = sk_ref.shape[1:3]
    halos = [
        push(sk_ref.at[:, nx - 1], hx.at[0], hs.at[0], hr.at[0], (row_up, col)),
        push(sk_ref.at[:, 0], hx.at[1], hs.at[1], hr.at[1], (row_down, col)),
        push(sk_ref.at[:, :, pl.ds(plane - 16, 16)], hy.at[0], hs.at[2], hr.at[2], (row, col_up)),
        push(sk_ref.at[:, :, pl.ds(0, 16)], hy.at[1], hs.at[3], hr.at[3], (row, col_down)),
    ]
    for copy in halos:
        copy.start()
    a1.wait_recv()
    acc1[...] = c_ref[core] + rc1[...]
    a2 = []
    for o in range(1, chips):
        q = chip_at(o)
        copy = push(acc1.at[q], rc2.at[chip], a2s.at[o], a2r.at[chip], on_chip(q))
        copy.start()
        a2.append(copy)

    extent, wide = diff.shape
    place = lax.broadcasted_iota(jnp.int32, (extent, wide), 0)
    diff[...] = (
        jnp.where(place == near_ref[0:1, :], 0.5, 0.0)
        - jnp.where(place == near_ref[1:2, :], 0.5, 0.0)
    ).astype(BF16)

    total = acc1[chip]
    for o in range(1, chips):
        q = chip_at(o)
        push(rc2.at[q], rc2.at[q], a2s.at[o], a2r.at[q], sibling).wait_recv()
        total = total + rc2[q]
    rc3[col] = total
    a3 = []
    for o in range(1, cols):
        copy = push(rc3.at[col], rc3.at[col], a3s.at[o], a3r.at[col], (row, col_at(o)))
        copy.start()
        a3.append(copy)
    for o in range(1, cols):
        z = col_at(o)
        push(rc3.at[z], rc3.at[z], a3s.at[o], a3r.at[z], sibling).wait_recv()
    total = rc3[0]
    for z in range(1, cols):
        total = total + rc3[z]
    cfull[core, chip] = total
    own = cfull.at[core, chip]
    a5 = [push(own, own, a5s.at[0], a5r.at[chip], sibling)]
    a4 = []
    for o in range(1, chips):
        copy = push(own, own, a4s.at[o], a4r.at[chip], on_chip(chip_at(o)))
        copy.start()
        a4.append(copy)
    a5[0].start()
    for o in range(1, chips):
        q = chip_at(o)
        block = cfull.at[core, q]
        push(block, block, a4s.at[o], a4r.at[q], sibling).wait_recv()
        copy = push(block, block, a5s.at[o], a5r.at[q], sibling)
        copy.start()
        a5.append(copy)
    for q in range(chips):
        block = cfull.at[1 - core, q]
        push(block, block, a5s.at[0], a5r.at[q], sibling).wait_recv()

    coeffs = cfull[...].reshape(-1, cfull.shape[-1])
    start = start_ref[...].T
    projected = jnp.dot(start, coeffs, precision=HIGHEST, preferred_element_type=F32)
    y_matrix = lax.dot_general(projected, coeffs, NT, precision=HIGHEST, preferred_element_type=F32)
    polar = y_matrix / jnp.sqrt(jnp.sum(y_matrix * y_matrix) + 1e-06)
    for _ in range(ITERS):
        gram = lax.dot_general(polar, polar, NT, precision=HIGHEST, preferred_element_type=F32)
        polar = 1.5 * polar - 0.5 * jnp.dot(
            gram, polar, precision=HIGHEST, preferred_element_type=F32
        )
    basis = polar.astype(BF16)
    modes, rank = basis.shape

    for copy in halos:
        copy.wait_recv()
    cells = nx * plane
    for c in range(3):
        inner = sk_ref[c].reshape(cells, rank)
        outer = jnp.concatenate(
            [hx[0, c], hx[1, c], hy[0, c].reshape(-1, rank), hy[1, c].reshape(-1, rank)], axis=0
        )
        field = lax.dot_general(basis, inner, NT, preferred_element_type=F32).astype(BF16)
        rim = lax.dot_general(basis, outer, NT, preferred_element_type=F32).astype(BF16)
        phi[c] = field.astype(F32).reshape(phi.shape[1:])
        phi_all[:, c * cells:(c + 1) * cells] = field
        slopes = jnp.dot(
            jnp.concatenate([field, rim], axis=1), diff[...], preferred_element_type=F32
        ).astype(BF16).astype(F32)
        for d in range(3):
            grad[d, c] = slopes[:, d * cells:(d + 1) * cells]

    blocks = gfull.shape[2]
    count = 128 * blocks // modes

    def part(which, q):
        group_at = which * chips + q
        for ct in range(cells // 128):
            lanes = slice(ct * 128, ct * 128 + 128)
            for group in range(0, count, 4):
                some = range(group, min(group + 4, count))
                p = [[phi[d, group_at, i:i + 1, lanes] for d in range(3)] for i in some]
                for c in range(3):
                    for jt in range(0, modes, 16):
                        g = [grad[d, c, jt:jt + 16, lanes] for d in range(3)]
                        for i, pi in zip(some, p):
                            adv[
                                i * modes + jt:i * modes + jt + 16,
                                c * cells + ct * 128:c * cells + ct * 128 + 128,
                            ] = (pi[0] * g[0] + pi[1] * g[1] + pi[2] * g[2]).astype(BF16)
        value = lax.dot_general(phi_all[...], adv[...], NT, preferred_element_type=F32)
        return [value[:, n * 128:n * 128 + 128] for n in range(blocks)]

    def theirs(step, carry):
        q = chip_at(step + 1)
        for n, value in enumerate(part(1 - core, q)):
            sg1[q, n] = value.astype(BF16)
        push(sg1.at[q], rg1.at[q], g1s.at[q], g1r.at[q], sibling).start()
        return carry

    lax.fori_loop(0, chips, theirs, 0)

    def ours(q):
        values = part(core, q)
        push(rg1.at[q], rg1.at[q], g1s.at[q], g1r.at[q], sibling).wait_recv()
        return [value + rg1[q, n].astype(F32) for n, value in enumerate(values)]

    def for_others(step, carry):
        q = chip_at(step + 1)
        for n, value in enumerate(ours(q)):
            sg2[q, n] = value.astype(BF16)
        push(sg2.at[q], rg2.at[chip], g2s.at[q], g2r.at[chip], on_chip(q)).start()
        return carry

    lax.fori_loop(0, chips - 1, for_others, 0)
    sums = ours(chip)
    for o in range(1, chips):
        q = chip_at(o)
        push(rg2.at[q], rg2.at[q], g2s.at[q], g2r.at[q], sibling).wait_recv()
        sums = [value + rg2[q, n].astype(F32) for n, value in enumerate(sums)]

    share = blocks // cols
    later = []
    if share:
        for n, value in enumerate(sums):
            sg3[n // share, n % share] = value.astype(BF16)
        for o in range(1, cols):
            z = col_at(o)
            copy = push(sg3.at[z], rg3.at[col], g3s.at[z], g3r.at[col], (row, z))
            copy.start()
            later.append(copy)
        final = sg3[col].astype(F32)
        for o in range(1, cols):
            z = col_at(o)
            push(rg3.at[z], rg3.at[z], g3s.at[z], g3r.at[z], sibling).wait_recv()
            final = final + rg3[z].astype(F32)
        own = gfull.at[core, chip, pl.ds(col * share, share)]
        own[...] = final.astype(BF16)
        for o in range(1, cols):
            z = col_at(o)
            copy = push(own, own, g4s.at[z], g4r.at[col], (row, z))
            copy.start()
            later.append(copy)
        for o in range(1, cols):
            z = col_at(o)
            block = gfull.at[core, chip, pl.ds(z * share, share)]
            push(block, block, g4s.at[z], g4r.at[z], sibling).wait_recv()
    else:
        for n, value in enumerate(sums):
            rg3[col, n] = value.astype(BF16)
        for o in range(1, cols):
            z = col_at(o)
            copy = push(rg3.at[col], rg3.at[col], g3s.at[z], g3r.at[col], (row, z))
            copy.start()
            later.append(copy)
        for o in range(1, cols):
            z = col_at(o)
            push(rg3.at[z], rg3.at[z], g3s.at[z], g3r.at[z], sibling).wait_recv()
        final = rg3[0].astype(F32)
        for z in range(1, cols):
            final = final + rg3[z].astype(F32)
        gfull[core, chip] = final.astype(BF16)

    own = gfull.at[core, chip]
    for o in range(1, chips):
        q = chip_at(o)
        copy = push(own, own, g5s.at[q], g5r.at[chip], on_chip(q))
        copy.start()
        later.append(copy)
    copy = push(own, own, g6s.at[chip], g6r.at[chip], sibling)
    copy.start()
    later.append(copy)

    def write(which, q):
        for n in range(blocks):
            at = pl.multiple_of(((which * chips + q) * blocks + n) * 128, 128)
            out_ref[:, pl.ds(at, 128)] = gfull[which, q, n].astype(F32) * scale

    write(core, chip)
    for o in range(1, chips):
        q = chip_at(o)
        block = gfull.at[core, q]
        push(block, block, g5s.at[q], g5r.at[q], sibling).wait_recv()
        copy = push(block, block, g6s.at[q], g6r.at[q], sibling)
        copy.start()
        later.append(copy)
        write(core, q)
    for o in range(chips):
        q = chip_at(o)
        block = gfull.at[1 - core, q]
        push(block, block, g6s.at[q], g6r.at[q], sibling).wait_recv()
        write(1 - core, q)

    for copy in [a1, *halos, *a2, *a3, *a4, *a5, *later]:
        copy.wait_send()
    for q in range(chips):
        push(sg1.at[q], rg1.at[q], g1s.at[q], g1r.at[q], sibling).wait_send()
    for o in range(1, chips):
        q = chip_at(o)
        push(sg2.at[q], rg2.at[q], g2s.at[q], g2r.at[q], sibling).wait_send()


def body(chips, cols, sketch, snapshots, start_block):
    nx, ny, nz, comps, rank = sketch.shape
    snaps = snapshots.shape[-1]
    modes = start_block.shape[1]
    cells = nx * ny * nz
    coeffs = lax.dot_general(
        sketch.reshape(cells * comps, rank), snapshots.reshape(cells * comps, snaps),
        (((0,), (0,)), ((), ())), preferred_element_type=F32,
    )
    depth = rank // (2 * chips)
    coeffs = coeffs.reshape(2, chips, depth, snaps)
    by_comp = sketch.transpose(3, 0, 1, 2, 4).reshape(comps, nx, ny * nz, rank)
    near = jnp.asarray(neighbour_columns(nx, ny, nz))
    extent = cells + 2 * ny * nz + 2 * nx * 16
    blocks = modes * modes // (2 * chips * 128)
    share = max(blocks // cols, 1)
    scale = 1.0 / math.sqrt(cells * 2 * chips * cols)
    counts = [4, 4, 1, 1] + [chips] * 2 + [cols] * 2 + [chips] * 4
    counts += [chips] * 4 + [cols] * 4 + [chips] * 4
    vmem = pl.BlockSpec(memory_space=pltpu.VMEM)
    return pl.pallas_call(
        functools.partial(kernel, chips, cols, scale),
        out_shape=jax.ShapeDtypeStruct((modes, modes * modes), F32),
        in_specs=[vmem] * 4,
        out_specs=vmem,
        scratch_shapes=[
            pltpu.VMEM((2, comps, ny * nz, rank), BF16),
            pltpu.VMEM((2, comps, nx, 16, rank), BF16),
            pltpu.VMEM((chips, depth, snaps), F32),
            pltpu.VMEM((chips, depth, snaps), F32),
            pltpu.VMEM((chips, depth, snaps), F32),
            pltpu.VMEM((cols, depth, snaps), F32),
            pltpu.VMEM((2, chips, depth, snaps), F32),
            pltpu.VMEM((extent, 3 * cells), BF16),
            pltpu.VMEM((comps, 2 * chips, modes // (2 * chips), cells), F32),
            pltpu.VMEM((modes, comps * cells), BF16),
            pltpu.VMEM((3, comps, modes, cells), F32),
            pltpu.VMEM((blocks * 128, comps * cells), BF16),
            pltpu.VMEM((chips, blocks, modes, 128), BF16),
            pltpu.VMEM((chips, blocks, modes, 128), BF16),
            pltpu.VMEM((chips, blocks, modes, 128), BF16),
            pltpu.VMEM((chips, blocks, modes, 128), BF16),
            pltpu.VMEM((cols, share, modes, 128), BF16),
            pltpu.VMEM((cols, share, modes, 128), BF16),
            pltpu.VMEM((2, chips, blocks, modes, 128), BF16),
        ] + [pltpu.SemaphoreType.DMA((n,)) for n in counts],
        compiler_params=pltpu.CompilerParams(
            collective_id=0, has_side_effects=True, vmem_limit_bytes=40 * 1024 * 1024
        ),
    )(coeffs, by_comp, start_block, near)


def solution(mesh):
    chips, cols = mesh.shape["row"] // 2, mesh.shape["col"]
    return jax.shard_map(
        functools.partial(body, chips, cols),
        mesh=mesh,
        in_specs=(P("row", "col", None, None, None), P("row", "col", None, None, None), P()),
        out_specs=P(),
        check_vma=False,
    )
```

```python
import functools
import math

import jax
import jax.numpy as jnp
from jax import lax
from jax.experimental import pallas as pl
from jax.experimental.pallas import tpu as pltpu
from jax.sharding import PartitionSpec as P

ITERS = 4
MESH = pl.DeviceIdType.MESH
F32 = jnp.float32
BF16 = jnp.bfloat16
HIGHEST = lax.Precision.HIGHEST
NT = (((1,), (1,)), ((), ()))


def neighbour_columns(nx, ny, nz):
    plane = ny * nz
    cells = nx * plane
    slab = 16
    cell = lax.broadcasted_iota(jnp.int32, (1, cells), 1)
    x, y, z = cell // plane, lax.rem(cell // nz, ny), lax.rem(cell, nz)
    x_before, x_after = cells, cells + plane
    y_before = cells + 2 * plane
    y_after = y_before + nx * slab
    ahead = [
        jnp.where(x < nx - 1, cell + plane, x_after + y * nz + z),
        jnp.where(y < ny - 1, cell + nz, y_after + x * slab + z),
        jnp.where(z < nz - 1, cell + 1, cell - (nz - 1)),
    ]
    behind = [
        jnp.where(x > 0, cell - plane, x_before + y * nz + z),
        jnp.where(y > 0, cell - nz, y_before + x * slab + slab - nz + z),
        jnp.where(z > 0, cell - 1, cell + nz - 1),
    ]
    return ahead, behind


def kernel(
    chips, cols, span, scale,
    flat_ref, snap_ref, sk_ref, start_ref, out_ref,
    sk_cols, hx, hy, sc1, rc1, acc1, rc2, rc3, cfull,
    diff, phi, phi_all, grad, adv,
    sg1, rg1, sg2, rg2, sg3, rg3, gfull,
    hs, hr, a1s, a1r, a2s, a2r, a3s, a3r, a4s, a4r, a5s, a5r,
    g1s, g1r, g2s, g2r, g3s, g3r, g4s, g4r, g5s, g5r, g6s, g6r,
):
    rows = 2 * chips
    row, col = lax.axis_index("row"), lax.axis_index("col")
    chip, core = row // 2, lax.rem(row, 2)
    sibling = (row + 1 - 2 * core, col)
    row_up, row_down = lax.rem(row + 1, rows), lax.rem(row + rows - 1, rows)
    col_up, col_down = lax.rem(col + 1, cols), lax.rem(col + cols - 1, cols)
    row_other = lax.rem(row + rows + 2 * core - 1, rows)

    def chip_at(offset):
        return lax.rem(chip + offset, chips)

    def col_at(offset):
        return lax.rem(col + offset, cols)

    def on_chip(q):
        return (2 * q + core, col)

    def push(src, dst, send, recv, device):
        return pltpu.make_async_remote_copy(
            src_ref=src, dst_ref=dst, send_sem=send, recv_sem=recv,
            device_id=device, device_id_type=MESH,
        )

    barrier = pltpu.get_barrier_semaphore()
    partners = [sibling, (row_other, col)]
    partners += [on_chip(chip_at(o)) for o in range(1, chips)]
    partners += [(row, col_at(o)) for o in range(1, cols)]
    for device in partners:
        pl.semaphore_signal(barrier, inc=1, device_id=device, device_id_type=MESH)

    sk_cols[...] = flat_ref[...].T.reshape(sk_cols.shape)

    def projection(which):
        half = jnp.dot(sk_cols[which], snap_ref[...], preferred_element_type=F32)
        return half.reshape(sc1.shape)

    sc1[...] = projection(1 - core)
    pl.semaphore_wait(barrier, len(partners))
    a1 = push(sc1, rc1, a1s.at[0], a1r.at[0], sibling)
    a1.start()
    nx, plane = sk_ref.shape[1:3]
    halos = [
        push(sk_ref.at[:, nx - 1], hx.at[0], hs.at[0], hr.at[0], (row_up, col)),
        push(sk_ref.at[:, 0], hx.at[1], hs.at[1], hr.at[1], (row_down, col)),
        push(sk_ref.at[:, :, pl.ds(plane - 16, 16)], hy.at[0], hs.at[2], hr.at[2], (row, col_up)),
        push(sk_ref.at[:, :, pl.ds(0, 16)], hy.at[1], hs.at[3], hr.at[3], (row, col_down)),
    ]
    for copy in halos:
        copy.start()
    mine = projection(core)
    a1.wait_recv()
    acc1[...] = mine + rc1[...]
    a2 = []
    for o in range(1, chips):
        q = chip_at(o)
        copy = push(acc1.at[q], rc2.at[chip], a2s.at[o], a2r.at[chip], on_chip(q))
        copy.start()
        a2.append(copy)

    extent = diff.shape[0]
    cells = nx * plane
    place = lax.broadcasted_iota(jnp.int32, (extent, cells), 0)
    for d, (fore, aft) in enumerate(zip(*neighbour_columns(nx, plane // span, span))):
        diff[:, d * cells:(d + 1) * cells] = (
            jnp.where(place == fore, 0.5, 0.0) - jnp.where(place == aft, 0.5, 0.0)
        ).astype(BF16)

    total = acc1[chip]
    for o in range(1, chips):
        q = chip_at(o)
        push(rc2.at[q], rc2.at[q], a2s.at[o], a2r.at[q], sibling).wait_recv()
        total = total + rc2[q]
    rc3[col] = total
    a3 = []
    for o in range(1, cols):
        copy = push(rc3.at[col], rc3.at[col], a3s.at[o], a3r.at[col], (row, col_at(o)))
        copy.start()
        a3.append(copy)
    for o in range(1, cols):
        z = col_at(o)
        push(rc3.at[z], rc3.at[z], a3s.at[o], a3r.at[z], sibling).wait_recv()
    total = rc3[0]
    for z in range(1, cols):
        total = total + rc3[z]
    cfull[core, chip] = total
    own = cfull.at[core, chip]
    a5 = [push(own, own, a5s.at[0], a5r.at[chip], sibling)]
    a4 = []
    for o in range(1, chips):
        copy = push(own, own, a4s.at[o], a4r.at[chip], on_chip(chip_at(o)))
        copy.start()
        a4.append(copy)
    a5[0].start()
    for o in range(1, chips):
        q = chip_at(o)
        block = cfull.at[core, q]
        push(block, block, a4s.at[o], a4r.at[q], sibling).wait_recv()
        copy = push(block, block, a5s.at[o], a5r.at[q], sibling)
        copy.start()
        a5.append(copy)
    for q in range(chips):
        block = cfull.at[1 - core, q]
        push(block, block, a5s.at[0], a5r.at[q], sibling).wait_recv()

    coeffs = cfull[...].reshape(-1, cfull.shape[-1])
    start = start_ref[...]
    projected = jnp.dot(start, coeffs, precision=HIGHEST, preferred_element_type=F32)
    y_matrix = lax.dot_general(projected, coeffs, NT, precision=HIGHEST, preferred_element_type=F32)
    polar = y_matrix / jnp.sqrt(jnp.sum(y_matrix * y_matrix) + 1e-06)
    for _ in range(ITERS):
        gram = lax.dot_general(polar, polar, NT, precision=HIGHEST, preferred_element_type=F32)
        polar = 1.5 * polar - 0.5 * jnp.dot(
            gram, polar, precision=HIGHEST, preferred_element_type=F32
        )
    basis = polar.astype(BF16)
    modes, rank = basis.shape

    for copy in halos:
        copy.wait_recv()
    for c in range(3):
        inner = sk_ref[c].reshape(cells, rank)
        outer = jnp.concatenate(
            [hx[0, c], hx[1, c], hy[0, c].reshape(-1, rank), hy[1, c].reshape(-1, rank)], axis=0
        )
        field = lax.dot_general(basis, inner, NT, preferred_element_type=F32).astype(BF16)
        rim = lax.dot_general(basis, outer, NT, preferred_element_type=F32).astype(BF16)
        phi[c] = field.astype(F32).reshape(phi.shape[1:])
        phi_all[:, c * cells:(c + 1) * cells] = field
        slopes = jnp.dot(
            jnp.concatenate([field, rim], axis=1), diff[...], preferred_element_type=F32
        ).astype(BF16).astype(F32)
        for d in range(3):
            grad[d, c] = slopes[:, d * cells:(d + 1) * cells]

    blocks = gfull.shape[2]
    count = 128 * blocks // modes

    def part(which, q):
        group_at = which * chips + q
        for ct in range(cells // 128):
            lanes = slice(ct * 128, ct * 128 + 128)
            for group in range(0, count, 4):
                some = range(group, min(group + 4, count))
                p = [[phi[d, group_at, i:i + 1, lanes] for d in range(3)] for i in some]
                for c in range(3):
                    for jt in range(0, modes, 16):
                        g = [grad[d, c, jt:jt + 16, lanes] for d in range(3)]
                        for i, pi in zip(some, p):
                            adv[
                                i * modes + jt:i * modes + jt + 16,
                                c * cells + ct * 128:c * cells + ct * 128 + 128,
                            ] = (pi[0] * g[0] + pi[1] * g[1] + pi[2] * g[2]).astype(BF16)
        value = lax.dot_general(phi_all[...], adv[...], NT, preferred_element_type=F32)
        return [value[:, n * 128:n * 128 + 128] for n in range(blocks)]

    def theirs(step, carry):
        q = chip_at(step + 1)
        for n, value in enumerate(part(1 - core, q)):
            sg1[q, n] = value.astype(BF16)
        push(sg1.at[q], rg1.at[q], g1s.at[q], g1r.at[q], sibling).start()
        return carry

    lax.fori_loop(0, chips, theirs, 0)

    def ours(q):
        values = part(core, q)
        push(rg1.at[q], rg1.at[q], g1s.at[q], g1r.at[q], sibling).wait_recv()
        return [value + rg1[q, n].astype(F32) for n, value in enumerate(values)]

    def for_others(step, carry):
        q = chip_at(step + 1)
        for n, value in enumerate(ours(q)):
            sg2[q, n] = value.astype(BF16)
        push(sg2.at[q], rg2.at[chip], g2s.at[q], g2r.at[chip], on_chip(q)).start()
        return carry

    lax.fori_loop(0, chips - 1, for_others, 0)
    sums = ours(chip)
    for o in range(1, chips):
        q = chip_at(o)
        push(rg2.at[q], rg2.at[q], g2s.at[q], g2r.at[q], sibling).wait_recv()
        sums = [value + rg2[q, n].astype(F32) for n, value in enumerate(sums)]

    share = blocks // cols
    later = []
    if share:
        for n, value in enumerate(sums):
            sg3[n // share, n % share] = value.astype(BF16)
        for o in range(1, cols):
            z = col_at(o)
            copy = push(sg3.at[z], rg3.at[col], g3s.at[z], g3r.at[col], (row, z))
            copy.start()
            later.append(copy)
        final = sg3[col].astype(F32)
        for o in range(1, cols):
            z = col_at(o)
            push(rg3.at[z], rg3.at[z], g3s.at[z], g3r.at[z], sibling).wait_recv()
            final = final + rg3[z].astype(F32)
        gfull[core, chip, pl.ds(col * share, share)] = final.astype(BF16)
        own = gfull.at[core, chip, pl.ds(col * share, share)]
        for o in range(1, cols):
            z = col_at(o)
            copy = push(own, own, g4s.at[z], g4r.at[col], (row, z))
            copy.start()
            later.append(copy)
    else:
        for n, value in enumerate(sums):
            rg3[col, n] = value.astype(BF16)
        for o in range(1, cols):
            z = col_at(o)
            copy = push(rg3.at[col], rg3.at[col], g3s.at[z], g3r.at[col], (row, z))
            copy.start()
            later.append(copy)
        for o in range(1, cols):
            z = col_at(o)
            push(rg3.at[z], rg3.at[z], g3s.at[z], g3r.at[z], sibling).wait_recv()
        final = rg3[0].astype(F32)
        for z in range(1, cols):
            final = final + rg3[z].astype(F32)
        gfull[core, chip] = final.astype(BF16)

    pieces = cols if share else 1
    width = blocks // pieces

    def piece(which, q, z):
        return gfull.at[which, q, pl.ds(z * width, width)]

    def write(which, q, z):
        for n in range(width):
            block = z * width + n
            at = pl.multiple_of(((which * chips + q) * blocks + block) * 128, 128)
            out_ref[:, pl.ds(at, 128)] = gfull[which, q, block].astype(F32) * scale

    def forward(q, z):
        part_of = piece(core, q, z)
        copy = push(part_of, part_of, g6s.at[q * pieces + z], g6r.at[q * pieces + z], sibling)
        copy.start()
        later.append(copy)
        write(core, q, z)

    order = [col_at(o) for o in range(pieces)] if share else [0]
    for o, z in enumerate(order):
        own = piece(core, chip, z)
        if o:
            push(own, own, g4s.at[z], g4r.at[z], sibling).wait_recv()
        for offset in range(1, chips):
            q = chip_at(offset)
            copy = push(
                own, own, g5s.at[q * pieces + z], g5r.at[chip * pieces + z], on_chip(q)
            )
            copy.start()
            later.append(copy)
        forward(chip, z)
    for z in order:
        for offset in range(1, chips):
            q = chip_at(offset)
            block = piece(core, q, z)
            slot = q * pieces + z
            push(block, block, g5s.at[slot], g5r.at[slot], sibling).wait_recv()
            forward(q, z)
    for z in order:
        for offset in range(chips):
            q = chip_at(offset)
            block = piece(1 - core, q, z)
            slot = q * pieces + z
            push(block, block, g6s.at[slot], g6r.at[slot], sibling).wait_recv()
            write(1 - core, q, z)

    for copy in [a1, *halos, *a2, *a3, *a4, *a5, *later]:
        copy.wait_send()
    for q in range(chips):
        push(sg1.at[q], rg1.at[q], g1s.at[q], g1r.at[q], sibling).wait_send()
    for o in range(1, chips):
        q = chip_at(o)
        push(sg2.at[q], rg2.at[q], g2s.at[q], g2r.at[q], sibling).wait_send()


def body(chips, cols, sketch, snapshots, start_block):
    nx, ny, nz, comps, rank = sketch.shape
    snaps = snapshots.shape[-1]
    modes = start_block.shape[1]
    cells = nx * ny * nz
    depth = rank // (2 * chips)
    flat = sketch.transpose(0, 1, 3, 2, 4).reshape(cells * comps, rank)
    snap = snapshots.transpose(0, 1, 3, 2, 4).reshape(cells * comps, snaps)
    by_comp = sketch.transpose(3, 0, 1, 2, 4).reshape(comps, nx, ny * nz, rank)
    extent = cells + 2 * ny * nz + 2 * nx * 16
    blocks = modes * modes // (2 * chips * 128)
    share = max(blocks // cols, 1)
    scale = 1.0 / math.sqrt(cells * 2 * chips * cols)
    counts = [4, 4, 1, 1] + [chips] * 2 + [cols] * 2 + [chips] * 4
    pieces = cols if blocks // cols else 1
    counts += [chips] * 4 + [cols] * 4 + [chips * pieces] * 4
    vmem = pl.BlockSpec(memory_space=pltpu.VMEM)
    return pl.pallas_call(
        functools.partial(kernel, chips, cols, nz, scale),
        out_shape=jax.ShapeDtypeStruct((modes, modes * modes), F32),
        in_specs=[vmem] * 4,
        out_specs=vmem,
        scratch_shapes=[
            pltpu.VMEM((2, rank // 2, comps * cells), BF16),
            pltpu.VMEM((2, comps, ny * nz, rank), BF16),
            pltpu.VMEM((2, comps, nx, 16, rank), BF16),
            pltpu.VMEM((chips, depth, snaps), F32),
            pltpu.VMEM((chips, depth, snaps), F32),
            pltpu.VMEM((chips, depth, snaps), F32),
            pltpu.VMEM((chips, depth, snaps), F32),
            pltpu.VMEM((cols, depth, snaps), F32),
            pltpu.VMEM((2, chips, depth, snaps), F32),
            pltpu.VMEM((extent, 3 * cells), BF16),
            pltpu.VMEM((comps, 2 * chips, modes // (2 * chips), cells), F32),
            pltpu.VMEM((modes, comps * cells), BF16),
            pltpu.VMEM((3, comps, modes, cells), F32),
            pltpu.VMEM((blocks * 128, comps * cells), BF16),
            pltpu.VMEM((chips, blocks, modes, 128), BF16),
            pltpu.VMEM((chips, blocks, modes, 128), BF16),
            pltpu.VMEM((chips, blocks, modes, 128), BF16),
            pltpu.VMEM((chips, blocks, modes, 128), BF16),
            pltpu.VMEM((cols, share, modes, 128), BF16),
            pltpu.VMEM((cols, share, modes, 128), BF16),
            pltpu.VMEM((2, chips, blocks, modes, 128), BF16),
        ] + [pltpu.SemaphoreType.DMA((n,)) for n in counts],
        compiler_params=pltpu.CompilerParams(
            collective_id=0, has_side_effects=True, vmem_limit_bytes=40 * 1024 * 1024
        ),
    )(flat, snap, by_comp, start_block.T)


def solution(mesh):
    chips, cols = mesh.shape["row"] // 2, mesh.shape["col"]
    return jax.shard_map(
        functools.partial(body, chips, cols),
        mesh=mesh,
        in_specs=(P("row", "col", None, None, None), P("row", "col", None, None, None), P()),
        out_specs=P(),
        check_vma=False,
    )
```

```python
import functools
import math

import jax
import jax.numpy as jnp
from jax import lax
from jax.experimental import pallas as pl
from jax.experimental.pallas import tpu as pltpu
from jax.sharding import PartitionSpec as P

ITERS = 4
MESH = pl.DeviceIdType.MESH
F32 = jnp.float32
BF16 = jnp.bfloat16
NT = (((1,), (1,)), ((), ()))


def neighbour_columns(nx, ny, nz):
    plane = ny * nz
    cells = nx * plane
    slab = 16
    cell = lax.broadcasted_iota(jnp.int32, (1, cells), 1)
    x, y, z = cell // plane, lax.rem(cell // nz, ny), lax.rem(cell, nz)
    x_before, x_after = cells, cells + plane
    y_before = cells + 2 * plane
    y_after = y_before + nx * slab
    ahead = [
        jnp.where(x < nx - 1, cell + plane, x_after + y * nz + z),
        jnp.where(y < ny - 1, cell + nz, y_after + x * slab + z),
        jnp.where(z < nz - 1, cell + 1, cell - (nz - 1)),
    ]
    behind = [
        jnp.where(x > 0, cell - plane, x_before + y * nz + z),
        jnp.where(y > 0, cell - nz, y_before + x * slab + slab - nz + z),
        jnp.where(z > 0, cell - 1, cell + nz - 1),
    ]
    return ahead, behind


def halves(value):
    high = value.astype(BF16)
    return high, (value - high.astype(F32)).astype(BF16)


def wide_left(value):
    high, low = halves(value)
    return jnp.concatenate([high, high, low], axis=1)


def kernel(
    chips, cols, span, scale,
    flat_ref, snap_ref, sk_ref, start_ref, out_ref,
    sk_cols, hx, hy, sc1, rc1, acc1, rc2, rc3, cfull,
    diff, phi, phi_all, grad, adv,
    sg1, rg1, sg2, rg2, sg3, rg3, gfull,
    hs, hr, a1s, a1r, a2s, a2r, a3s, a3r, a4s, a4r, a5s, a5r,
    g1s, g1r, g2s, g2r, g3s, g3r, g4s, g4r, g5s, g5r, g6s, g6r,
):
    rows = 2 * chips
    row, col = lax.axis_index("row"), lax.axis_index("col")
    chip, core = row // 2, lax.rem(row, 2)
    sibling = (row + 1 - 2 * core, col)
    row_up, row_down = lax.rem(row + 1, rows), lax.rem(row + rows - 1, rows)
    col_up, col_down = lax.rem(col + 1, cols), lax.rem(col + cols - 1, cols)
    row_other = lax.rem(row + rows + 2 * core - 1, rows)

    def chip_at(offset):
        return lax.rem(chip + offset, chips)

    def col_at(offset):
        return lax.rem(col + offset, cols)

    def on_chip(q):
        return (2 * q + core, col)

    def push(src, dst, send, recv, device):
        return pltpu.make_async_remote_copy(
            src_ref=src, dst_ref=dst, send_sem=send, recv_sem=recv,
            device_id=device, device_id_type=MESH,
        )

    barrier = pltpu.get_barrier_semaphore()
    partners = [sibling, (row_other, col)]
    partners += [on_chip(chip_at(o)) for o in range(1, chips)]
    partners += [(row, col_at(o)) for o in range(1, cols)]
    for device in partners:
        pl.semaphore_signal(barrier, inc=1, device_id=device, device_id_type=MESH)

    sk_cols[...] = flat_ref[...].T.reshape(sk_cols.shape)

    def projection(which):
        half = jnp.dot(sk_cols[which], snap_ref[...], preferred_element_type=F32)
        return half.reshape(sc1.shape)

    sc1[...] = projection(1 - core)
    pl.semaphore_wait(barrier, len(partners))
    a1 = push(sc1, rc1, a1s.at[0], a1r.at[0], sibling)
    a1.start()
    nx, plane = sk_ref.shape[1:3]
    halos = [
        push(sk_ref.at[:, nx - 1], hx.at[0], hs.at[0], hr.at[0], (row_up, col)),
        push(sk_ref.at[:, 0], hx.at[1], hs.at[1], hr.at[1], (row_down, col)),
        push(sk_ref.at[:, :, pl.ds(plane - 16, 16)], hy.at[0], hs.at[2], hr.at[2], (row, col_up)),
        push(sk_ref.at[:, :, pl.ds(0, 16)], hy.at[1], hs.at[3], hr.at[3], (row, col_down)),
    ]
    for copy in halos:
        copy.start()
    mine = projection(core)
    a1.wait_recv()
    acc1[...] = mine + rc1[...]
    a2 = []
    for o in range(1, chips):
        q = chip_at(o)
        copy = push(acc1.at[q], rc2.at[chip], a2s.at[o], a2r.at[chip], on_chip(q))
        copy.start()
        a2.append(copy)

    extent = diff.shape[0]
    cells = nx * plane
    place = lax.broadcasted_iota(jnp.int32, (extent, cells), 0)
    for d, (fore, aft) in enumerate(zip(*neighbour_columns(nx, plane // span, span))):
        diff[:, d * cells:(d + 1) * cells] = (
            jnp.where(place == fore, 0.5, 0.0) - jnp.where(place == aft, 0.5, 0.0)
        ).astype(BF16)

    total = acc1[chip]
    for o in range(1, chips):
        q = chip_at(o)
        push(rc2.at[q], rc2.at[q], a2s.at[o], a2r.at[q], sibling).wait_recv()
        total = total + rc2[q]
    rc3[col] = total
    a3 = []
    for o in range(1, cols):
        copy = push(rc3.at[col], rc3.at[col], a3s.at[o], a3r.at[col], (row, col_at(o)))
        copy.start()
        a3.append(copy)
    for o in range(1, cols):
        z = col_at(o)
        push(rc3.at[z], rc3.at[z], a3s.at[o], a3r.at[z], sibling).wait_recv()
    total = rc3[0]
    for z in range(1, cols):
        total = total + rc3[z]
    cfull[core, chip] = total
    own = cfull.at[core, chip]
    a5 = [push(own, own, a5s.at[0], a5r.at[chip], sibling)]
    a4 = []
    for o in range(1, chips):
        copy = push(own, own, a4s.at[o], a4r.at[chip], on_chip(chip_at(o)))
        copy.start()
        a4.append(copy)
    a5[0].start()
    for o in range(1, chips):
        q = chip_at(o)
        block = cfull.at[core, q]
        push(block, block, a4s.at[o], a4r.at[q], sibling).wait_recv()
        copy = push(block, block, a5s.at[o], a5r.at[q], sibling)
        copy.start()
        a5.append(copy)
    for q in range(chips):
        block = cfull.at[1 - core, q]
        push(block, block, a5s.at[0], a5r.at[q], sibling).wait_recv()

    coeffs = cfull[...].reshape(-1, cfull.shape[-1])
    start = start_ref[...]
    modes, rank = start.shape
    coeffs_h, coeffs_l = halves(coeffs)
    projected = jnp.dot(
        wide_left(start),
        jnp.concatenate([coeffs_h, coeffs_l, coeffs_h], axis=0),
        preferred_element_type=F32,
    )
    y_matrix = lax.dot_general(
        wide_left(projected),
        jnp.concatenate([coeffs_h, coeffs_l, coeffs_h], axis=1),
        NT, preferred_element_type=F32,
    )
    polar = y_matrix / jnp.sqrt(jnp.sum(y_matrix * y_matrix) + 1e-06)
    polar = jnp.concatenate([polar, jnp.zeros((-modes % 128, rank), F32)], axis=0)
    for _ in range(ITERS):
        high, low = halves(polar)
        gram = lax.dot_general(
            jnp.concatenate([high, high, low], axis=1),
            jnp.concatenate([high, low, high], axis=1),
            NT, preferred_element_type=F32,
        )
        polar = 1.5 * polar - 0.5 * jnp.dot(
            wide_left(gram),
            jnp.concatenate([high, low, high], axis=0),
            preferred_element_type=F32,
        )
    polar = polar[:modes]
    basis = polar.astype(BF16)

    for copy in halos:
        copy.wait_recv()
    for c in range(3):
        inner = sk_ref[c].reshape(cells, rank)
        outer = jnp.concatenate(
            [hx[0, c], hx[1, c], hy[0, c].reshape(-1, rank), hy[1, c].reshape(-1, rank)], axis=0
        )
        field = lax.dot_general(basis, inner, NT, preferred_element_type=F32).astype(BF16)
        rim = lax.dot_general(basis, outer, NT, preferred_element_type=F32).astype(BF16)
        phi[c] = field.astype(F32).reshape(phi.shape[1:])
        phi_all[:, c * cells:(c + 1) * cells] = field
        slopes = jnp.dot(
            jnp.concatenate([field, rim], axis=1), diff[...], preferred_element_type=F32
        ).astype(BF16)
        for d in range(3):
            grad[d, c] = slopes[:, d * cells:(d + 1) * cells]

    blocks = gfull.shape[2]
    count = 128 * blocks // modes

    def part(which, q):
        group_at = which * chips + q
        for ct in range(cells // 128):
            lanes = slice(ct * 128, ct * 128 + 128)
            for group in range(0, count, 4):
                some = range(group, min(group + 4, count))
                p = [
                    [
                        jnp.broadcast_to(phi[d, group_at, i:i + 1, lanes], (16, 128)).astype(BF16)
                        for d in range(3)
                    ]
                    for i in some
                ]
                for c in range(3):
                    for jt in range(0, modes, 16):
                        g = [grad[d, c, jt:jt + 16, lanes] for d in range(3)]
                        for i, pi in zip(some, p):
                            adv[
                                i * modes + jt:i * modes + jt + 16,
                                c * cells + ct * 128:c * cells + ct * 128 + 128,
                            ] = pi[0] * g[0] + pi[1] * g[1] + pi[2] * g[2]
        value = lax.dot_general(phi_all[...], adv[...], NT, preferred_element_type=F32)
        return [value[:, n * 128:n * 128 + 128] for n in range(blocks)]

    def theirs(step, carry):
        q = chip_at(step + 1)
        for n, value in enumerate(part(1 - core, q)):
            sg1[q, n] = value.astype(BF16)
        push(sg1.at[q], rg1.at[q], g1s.at[q], g1r.at[q], sibling).start()
        return carry

    lax.fori_loop(0, chips, theirs, 0)

    def ours(q):
        values = part(core, q)
        push(rg1.at[q], rg1.at[q], g1s.at[q], g1r.at[q], sibling).wait_recv()
        return [value + rg1[q, n].astype(F32) for n, value in enumerate(values)]

    def for_others(step, carry):
        q = chip_at(step + 1)
        for n, value in enumerate(ours(q)):
            sg2[q, n] = value.astype(BF16)
        push(sg2.at[q], rg2.at[chip], g2s.at[q], g2r.at[chip], on_chip(q)).start()
        return carry

    lax.fori_loop(0, chips - 1, for_others, 0)
    sums = ours(chip)
    for o in range(1, chips):
        q = chip_at(o)
        push(rg2.at[q], rg2.at[q], g2s.at[q], g2r.at[q], sibling).wait_recv()
        sums = [value + rg2[q, n].astype(F32) for n, value in enumerate(sums)]

    share = blocks // cols
    later = []
    if share:
        for n, value in enumerate(sums):
            sg3[n // share, n % share] = value.astype(BF16)
        for o in range(1, cols):
            z = col_at(o)
            copy = push(sg3.at[z], rg3.at[col], g3s.at[z], g3r.at[col], (row, z))
            copy.start()
            later.append(copy)
        final = sg3[col].astype(F32)
        for o in range(1, cols):
            z = col_at(o)
            push(rg3.at[z], rg3.at[z], g3s.at[z], g3r.at[z], sibling).wait_recv()
            final = final + rg3[z].astype(F32)
        gfull[core, chip, pl.ds(col * share, share)] = final.astype(BF16)
        own = gfull.at[core, chip, pl.ds(col * share, share)]
        for o in range(1, cols):
            z = col_at(o)
            copy = push(own, own, g4s.at[z], g4r.at[col], (row, z))
            copy.start()
            later.append(copy)
    else:
        for n, value in enumerate(sums):
            rg3[col, n] = value.astype(BF16)
        for o in range(1, cols):
            z = col_at(o)
            copy = push(rg3.at[col], rg3.at[col], g3s.at[z], g3r.at[col], (row, z))
            copy.start()
            later.append(copy)
        for o in range(1, cols):
            z = col_at(o)
            push(rg3.at[z], rg3.at[z], g3s.at[z], g3r.at[z], sibling).wait_recv()
        final = rg3[0].astype(F32)
        for z in range(1, cols):
            final = final + rg3[z].astype(F32)
        gfull[core, chip] = final.astype(BF16)

    pieces = cols if share else 1
    width = blocks // pieces

    def piece(which, q, z):
        return gfull.at[which, q, pl.ds(z * width, width)]

    def write(which, q, z):
        for n in range(width):
            block = z * width + n
            at = pl.multiple_of(((which * chips + q) * blocks + block) * 128, 128)
            out_ref[:, pl.ds(at, 128)] = gfull[which, q, block].astype(F32) * scale

    def forward(q, z):
        part_of = piece(core, q, z)
        copy = push(part_of, part_of, g6s.at[q * pieces + z], g6r.at[q * pieces + z], sibling)
        copy.start()
        later.append(copy)
        write(core, q, z)

    order = [col_at(o) for o in range(pieces)] if share else [0]
    for o, z in enumerate(order):
        own = piece(core, chip, z)
        if o:
            push(own, own, g4s.at[z], g4r.at[z], sibling).wait_recv()
        for offset in range(1, chips):
            q = chip_at(offset)
            copy = push(
                own, own, g5s.at[q * pieces + z], g5r.at[chip * pieces + z], on_chip(q)
            )
            copy.start()
            later.append(copy)
        forward(chip, z)
    for z in order:
        for offset in range(1, chips):
            q = chip_at(offset)
            block = piece(core, q, z)
            slot = q * pieces + z
            push(block, block, g5s.at[slot], g5r.at[slot], sibling).wait_recv()
            forward(q, z)
    for z in order:
        for offset in range(chips):
            q = chip_at(offset)
            block = piece(1 - core, q, z)
            slot = q * pieces + z
            push(block, block, g6s.at[slot], g6r.at[slot], sibling).wait_recv()
            write(1 - core, q, z)

    for copy in [a1, *halos, *a2, *a3, *a4, *a5, *later]:
        copy.wait_send()
    for q in range(chips):
        push(sg1.at[q], rg1.at[q], g1s.at[q], g1r.at[q], sibling).wait_send()
    for o in range(1, chips):
        q = chip_at(o)
        push(sg2.at[q], rg2.at[q], g2s.at[q], g2r.at[q], sibling).wait_send()


def body(chips, cols, sketch, snapshots, start_block):
    nx, ny, nz, comps, rank = sketch.shape
    snaps = snapshots.shape[-1]
    modes = start_block.shape[1]
    cells = nx * ny * nz
    depth = rank // (2 * chips)
    flat = sketch.transpose(0, 1, 3, 2, 4).reshape(cells * comps, rank)
    snap = snapshots.transpose(0, 1, 3, 2, 4).reshape(cells * comps, snaps)
    by_comp = sketch.transpose(3, 0, 1, 2, 4).reshape(comps, nx, ny * nz, rank)
    extent = cells + 2 * ny * nz + 2 * nx * 16
    blocks = modes * modes // (2 * chips * 128)
    share = max(blocks // cols, 1)
    scale = 1.0 / math.sqrt(cells * 2 * chips * cols)
    counts = [4, 4, 1, 1] + [chips] * 2 + [cols] * 2 + [chips] * 4
    pieces = cols if blocks // cols else 1
    counts += [chips] * 4 + [cols] * 4 + [chips * pieces] * 4
    vmem = pl.BlockSpec(memory_space=pltpu.VMEM)
    return pl.pallas_call(
        functools.partial(kernel, chips, cols, nz, scale),
        out_shape=jax.ShapeDtypeStruct((modes, modes * modes), F32),
        in_specs=[vmem] * 4,
        out_specs=vmem,
        scratch_shapes=[
            pltpu.VMEM((2, rank // 2, comps * cells), BF16),
            pltpu.VMEM((2, comps, ny * nz, rank), BF16),
            pltpu.VMEM((2, comps, nx, 16, rank), BF16),
            pltpu.VMEM((chips, depth, snaps), F32),
            pltpu.VMEM((chips, depth, snaps), F32),
            pltpu.VMEM((chips, depth, snaps), F32),
            pltpu.VMEM((chips, depth, snaps), F32),
            pltpu.VMEM((cols, depth, snaps), F32),
            pltpu.VMEM((2, chips, depth, snaps), F32),
            pltpu.VMEM((extent, 3 * cells), BF16),
            pltpu.VMEM((comps, 2 * chips, modes // (2 * chips), cells), F32),
            pltpu.VMEM((modes, comps * cells), BF16),
            pltpu.VMEM((3, comps, modes, cells), BF16),
            pltpu.VMEM((blocks * 128, comps * cells), BF16),
            pltpu.VMEM((chips, blocks, modes, 128), BF16),
            pltpu.VMEM((chips, blocks, modes, 128), BF16),
            pltpu.VMEM((chips, blocks, modes, 128), BF16),
            pltpu.VMEM((chips, blocks, modes, 128), BF16),
            pltpu.VMEM((cols, share, modes, 128), BF16),
            pltpu.VMEM((cols, share, modes, 128), BF16),
            pltpu.VMEM((2, chips, blocks, modes, 128), BF16),
        ] + [pltpu.SemaphoreType.DMA((n,)) for n in counts],
        compiler_params=pltpu.CompilerParams(
            collective_id=0, has_side_effects=True, vmem_limit_bytes=40 * 1024 * 1024
        ),
    )(flat, snap, by_comp, start_block.T)


def solution(mesh):
    chips, cols = mesh.shape["row"] // 2, mesh.shape["col"]
    return jax.shard_map(
        functools.partial(body, chips, cols),
        mesh=mesh,
        in_specs=(P("row", "col", None, None, None), P("row", "col", None, None, None), P()),
        out_specs=P(),
        check_vma=False,
    )
```

```python
import functools
import math

import jax
import jax.numpy as jnp
from jax import lax
from jax.experimental import pallas as pl
from jax.experimental.pallas import tpu as pltpu
from jax.sharding import PartitionSpec as P

ITERS = 4
MESH = pl.DeviceIdType.MESH
F32 = jnp.float32
BF16 = jnp.bfloat16
NT = (((1,), (1,)), ((), ()))


def neighbour_columns(nx, ny, nz):
    plane = ny * nz
    cells = nx * plane
    slab = 16
    cell = lax.broadcasted_iota(jnp.int32, (1, cells), 1)
    x, y, z = cell // plane, lax.rem(cell // nz, ny), lax.rem(cell, nz)
    x_before, x_after = cells, cells + plane
    y_before = cells + 2 * plane
    y_after = y_before + nx * slab
    ahead = [
        jnp.where(x < nx - 1, cell + plane, x_after + y * nz + z),
        jnp.where(y < ny - 1, cell + nz, y_after + x * slab + z),
        jnp.where(z < nz - 1, cell + 1, cell - (nz - 1)),
    ]
    behind = [
        jnp.where(x > 0, cell - plane, x_before + y * nz + z),
        jnp.where(y > 0, cell - nz, y_before + x * slab + slab - nz + z),
        jnp.where(z > 0, cell - 1, cell + nz - 1),
    ]
    return ahead, behind


def halves(value):
    high = value.astype(BF16)
    return high, (value - high.astype(F32)).astype(BF16)


def wide_left(value):
    high, low = halves(value)
    return jnp.concatenate([high, high, low], axis=1)


def kernel(
    chips, cols, span, scale,
    lie_hbm, snap_hbm, start_hbm, out_ref,
    lie_ref, snap_ref, start_ref, loads, sk_ref, sk_cols, hx, hy, sc1, rc1, acc1, rc2, rc3, cfull,
    diff, phi, phi_all, grad, adv,
    sg1, rg1, sg2, rg2, sg3, rg3, gfull,
    hs, hr, a1s, a1r, a2s, a2r, a3s, a3r, a4s, a4r, a5s, a5r,
    g1s, g1r, g2s, g2r, g3s, g3r, g4s, g4r, g5s, g5r, g6s, g6r,
):
    rows = 2 * chips
    row, col = lax.axis_index("row"), lax.axis_index("col")
    chip, core = row // 2, lax.rem(row, 2)
    sibling = (row + 1 - 2 * core, col)
    row_up, row_down = lax.rem(row + 1, rows), lax.rem(row + rows - 1, rows)
    col_up, col_down = lax.rem(col + 1, cols), lax.rem(col + cols - 1, cols)
    row_other = lax.rem(row + rows + 2 * core - 1, rows)

    def chip_at(offset):
        return lax.rem(chip + offset, chips)

    def col_at(offset):
        return lax.rem(col + offset, cols)

    def on_chip(q):
        return (2 * q + core, col)

    def push(src, dst, send, recv, device):
        return pltpu.make_async_remote_copy(
            src_ref=src, dst_ref=dst, send_sem=send, recv_sem=recv,
            device_id=device, device_id_type=MESH,
        )

    fetches = [
        pltpu.make_async_copy(src, dst, loads.at[n])
        for n, (src, dst) in enumerate(
            [(snap_hbm, snap_ref), (lie_hbm, lie_ref), (start_hbm, start_ref)]
        )
    ]
    for copy in fetches:
        copy.start()
    barrier = pltpu.get_barrier_semaphore()
    partners = [sibling, (row_other, col)]
    partners += [on_chip(chip_at(o)) for o in range(1, chips)]
    partners += [(row, col_at(o)) for o in range(1, cols)]
    for device in partners:
        pl.semaphore_signal(barrier, inc=1, device_id=device, device_id_type=MESH)

    comps, rank = sk_ref.shape[0], sk_ref.shape[-1]
    for copy in fetches:
        copy.wait()
    snaps = snap_ref[...].reshape(-1, snap_ref.shape[-1])
    sk_cols[...] = lie_ref[...].reshape(-1, rank).T.reshape(sk_cols.shape)
    for c in range(comps):
        sk_ref[c] = lie_ref[:, c].reshape(sk_ref.shape[1:])

    def projection(which):
        half = jnp.dot(sk_cols[which], snaps, preferred_element_type=F32)
        return half.reshape(sc1.shape)

    sc1[...] = projection(1 - core)
    pl.semaphore_wait(barrier, len(partners))
    a1 = push(sc1, rc1, a1s.at[0], a1r.at[0], sibling)
    a1.start()
    nx, plane = sk_ref.shape[1:3]
    halos = [
        push(sk_ref.at[:, nx - 1], hx.at[0], hs.at[0], hr.at[0], (row_up, col)),
        push(sk_ref.at[:, 0], hx.at[1], hs.at[1], hr.at[1], (row_down, col)),
        push(sk_ref.at[:, :, pl.ds(plane - 16, 16)], hy.at[0], hs.at[2], hr.at[2], (row, col_up)),
        push(sk_ref.at[:, :, pl.ds(0, 16)], hy.at[1], hs.at[3], hr.at[3], (row, col_down)),
    ]
    for copy in halos:
        copy.start()
    mine = projection(core)
    a1.wait_recv()
    acc1[...] = mine + rc1[...]
    a2 = []
    for o in range(1, chips):
        q = chip_at(o)
        copy = push(acc1.at[q], rc2.at[chip], a2s.at[o], a2r.at[chip], on_chip(q))
        copy.start()
        a2.append(copy)

    extent = diff.shape[0]
    cells = nx * plane
    place = lax.broadcasted_iota(jnp.int32, (extent, cells), 0)
    for d, (fore, aft) in enumerate(zip(*neighbour_columns(nx, plane // span, span))):
        diff[:, d * cells:(d + 1) * cells] = (
            jnp.where(place == fore, 0.5, 0.0) - jnp.where(place == aft, 0.5, 0.0)
        ).astype(BF16)

    total = acc1[chip]
    for o in range(1, chips):
        q = chip_at(o)
        push(rc2.at[q], rc2.at[q], a2s.at[o], a2r.at[q], sibling).wait_recv()
        total = total + rc2[q]
    rc3[col] = total
    a3 = []
    for o in range(1, cols):
        copy = push(rc3.at[col], rc3.at[col], a3s.at[o], a3r.at[col], (row, col_at(o)))
        copy.start()
        a3.append(copy)
    for o in range(1, cols):
        z = col_at(o)
        push(rc3.at[z], rc3.at[z], a3s.at[o], a3r.at[z], sibling).wait_recv()
    total = rc3[0]
    for z in range(1, cols):
        total = total + rc3[z]
    cfull[core, chip] = total
    own = cfull.at[core, chip]
    a5 = [push(own, own, a5s.at[0], a5r.at[chip], sibling)]
    a4 = []
    for o in range(1, chips):
        copy = push(own, own, a4s.at[o], a4r.at[chip], on_chip(chip_at(o)))
        copy.start()
        a4.append(copy)
    a5[0].start()
    for o in range(1, chips):
        q = chip_at(o)
        block = cfull.at[core, q]
        push(block, block, a4s.at[o], a4r.at[q], sibling).wait_recv()
        copy = push(block, block, a5s.at[o], a5r.at[q], sibling)
        copy.start()
        a5.append(copy)
    for q in range(chips):
        block = cfull.at[1 - core, q]
        push(block, block, a5s.at[0], a5r.at[q], sibling).wait_recv()

    coeffs = cfull[...].reshape(-1, cfull.shape[-1])
    start = start_ref[...]
    modes, rank = start.shape
    coeffs_h, coeffs_l = halves(coeffs)
    projected = jnp.dot(
        wide_left(start),
        jnp.concatenate([coeffs_h, coeffs_l, coeffs_h], axis=0),
        preferred_element_type=F32,
    )
    y_matrix = lax.dot_general(
        wide_left(projected),
        jnp.concatenate([coeffs_h, coeffs_l, coeffs_h], axis=1),
        NT, preferred_element_type=F32,
    )
    polar = y_matrix / jnp.sqrt(jnp.sum(y_matrix * y_matrix) + 1e-06)
    polar = jnp.concatenate([polar, jnp.zeros((-modes % 128, rank), F32)], axis=0)
    for _ in range(ITERS):
        high, low = halves(polar)
        gram = lax.dot_general(
            jnp.concatenate([high, high, low], axis=1),
            jnp.concatenate([high, low, high], axis=1),
            NT, preferred_element_type=F32,
        )
        polar = 1.5 * polar - 0.5 * jnp.dot(
            wide_left(gram),
            jnp.concatenate([high, low, high], axis=0),
            preferred_element_type=F32,
        )
    polar = polar[:modes]
    basis = polar.astype(BF16)

    for copy in halos:
        copy.wait_recv()
    for c in range(3):
        inner = sk_ref[c].reshape(cells, rank)
        outer = jnp.concatenate(
            [hx[0, c], hx[1, c], hy[0, c].reshape(-1, rank), hy[1, c].reshape(-1, rank)], axis=0
        )
        field = lax.dot_general(basis, inner, NT, preferred_element_type=F32).astype(BF16)
        rim = lax.dot_general(basis, outer, NT, preferred_element_type=F32).astype(BF16)
        phi[c] = field.astype(F32).reshape(phi.shape[1:])
        phi_all[:, c * cells:(c + 1) * cells] = field
        slopes = jnp.dot(
            jnp.concatenate([field, rim], axis=1), diff[...], preferred_element_type=F32
        ).astype(BF16)
        for d in range(3):
            grad[d, c] = slopes[:, d * cells:(d + 1) * cells]

    blocks = gfull.shape[2]
    count = 128 * blocks // modes

    def part(which, q):
        group_at = which * chips + q
        for ct in range(cells // 128):
            lanes = slice(ct * 128, ct * 128 + 128)
            for group in range(0, count, 4):
                some = range(group, min(group + 4, count))
                p = [
                    [
                        jnp.broadcast_to(phi[d, group_at, i:i + 1, lanes], (16, 128)).astype(BF16)
                        for d in range(3)
                    ]
                    for i in some
                ]
                for c in range(3):
                    for jt in range(0, modes, 16):
                        g = [grad[d, c, jt:jt + 16, lanes] for d in range(3)]
                        for i, pi in zip(some, p):
                            adv[
                                i * modes + jt:i * modes + jt + 16,
                                c * cells + ct * 128:c * cells + ct * 128 + 128,
                            ] = pi[0] * g[0] + pi[1] * g[1] + pi[2] * g[2]
        value = lax.dot_general(phi_all[...], adv[...], NT, preferred_element_type=F32)
        return [value[:, n * 128:n * 128 + 128] for n in range(blocks)]

    def theirs(step, carry):
        q = chip_at(step + 1)
        for n, value in enumerate(part(1 - core, q)):
            sg1[q, n] = value.astype(BF16)
        push(sg1.at[q], rg1.at[q], g1s.at[q], g1r.at[q], sibling).start()
        return carry

    lax.fori_loop(0, chips, theirs, 0)

    def ours(q):
        values = part(core, q)
        push(rg1.at[q], rg1.at[q], g1s.at[q], g1r.at[q], sibling).wait_recv()
        return [value + rg1[q, n].astype(F32) for n, value in enumerate(values)]

    def for_others(step, carry):
        q = chip_at(step + 1)
        for n, value in enumerate(ours(q)):
            sg2[q, n] = value.astype(BF16)
        push(sg2.at[q], rg2.at[chip], g2s.at[q], g2r.at[chip], on_chip(q)).start()
        return carry

    lax.fori_loop(0, chips - 1, for_others, 0)
    sums = ours(chip)
    for o in range(1, chips):
        q = chip_at(o)
        push(rg2.at[q], rg2.at[q], g2s.at[q], g2r.at[q], sibling).wait_recv()
        sums = [value + rg2[q, n].astype(F32) for n, value in enumerate(sums)]

    share = blocks // cols
    later = []
    if share:
        for n, value in enumerate(sums):
            sg3[n // share, n % share] = value.astype(BF16)
        for o in range(1, cols):
            z = col_at(o)
            copy = push(sg3.at[z], rg3.at[col], g3s.at[z], g3r.at[col], (row, z))
            copy.start()
            later.append(copy)
        final = sg3[col].astype(F32)
        for o in range(1, cols):
            z = col_at(o)
            push(rg3.at[z], rg3.at[z], g3s.at[z], g3r.at[z], sibling).wait_recv()
            final = final + rg3[z].astype(F32)
        gfull[core, chip, pl.ds(col * share, share)] = final.astype(BF16)
        own = gfull.at[core, chip, pl.ds(col * share, share)]
        for o in range(1, cols):
            z = col_at(o)
            copy = push(own, own, g4s.at[z], g4r.at[col], (row, z))
            copy.start()
            later.append(copy)
    else:
        for n, value in enumerate(sums):
            rg3[col, n] = value.astype(BF16)
        for o in range(1, cols):
            z = col_at(o)
            copy = push(rg3.at[col], rg3.at[col], g3s.at[z], g3r.at[col], (row, z))
            copy.start()
            later.append(copy)
        for o in range(1, cols):
            z = col_at(o)
            push(rg3.at[z], rg3.at[z], g3s.at[z], g3r.at[z], sibling).wait_recv()
        final = rg3[0].astype(F32)
        for z in range(1, cols):
            final = final + rg3[z].astype(F32)
        gfull[core, chip] = final.astype(BF16)

    pieces = cols if share else 1
    width = blocks // pieces

    def piece(which, q, z):
        return gfull.at[which, q, pl.ds(z * width, width)]

    def write(which, q, z):
        for n in range(width):
            block = z * width + n
            at = pl.multiple_of(((which * chips + q) * blocks + block) * 128, 128)
            out_ref[:, pl.ds(at, 128)] = gfull[which, q, block].astype(F32) * scale

    def forward(q, z):
        part_of = piece(core, q, z)
        copy = push(part_of, part_of, g6s.at[q * pieces + z], g6r.at[q * pieces + z], sibling)
        copy.start()
        later.append(copy)
        write(core, q, z)

    order = [col_at(o) for o in range(pieces)] if share else [0]
    for o, z in enumerate(order):
        own = piece(core, chip, z)
        if o:
            push(own, own, g4s.at[z], g4r.at[z], sibling).wait_recv()
        for offset in range(1, chips):
            q = chip_at(offset)
            copy = push(
                own, own, g5s.at[q * pieces + z], g5r.at[chip * pieces + z], on_chip(q)
            )
            copy.start()
            later.append(copy)
        forward(chip, z)
    for z in order:
        for offset in range(1, chips):
            q = chip_at(offset)
            block = piece(core, q, z)
            slot = q * pieces + z
            push(block, block, g5s.at[slot], g5r.at[slot], sibling).wait_recv()
            forward(q, z)
    for z in order:
        for offset in range(chips):
            q = chip_at(offset)
            block = piece(1 - core, q, z)
            slot = q * pieces + z
            push(block, block, g6s.at[slot], g6r.at[slot], sibling).wait_recv()
            write(1 - core, q, z)

    for copy in [a1, *halos, *a2, *a3, *a4, *a5, *later]:
        copy.wait_send()
    for q in range(chips):
        push(sg1.at[q], rg1.at[q], g1s.at[q], g1r.at[q], sibling).wait_send()
    for o in range(1, chips):
        q = chip_at(o)
        push(sg2.at[q], rg2.at[q], g2s.at[q], g2r.at[q], sibling).wait_send()


def body(chips, cols, sketch, snapshots, start_block):
    nx, ny, nz, comps, rank = sketch.shape
    snaps = snapshots.shape[-1]
    modes = start_block.shape[1]
    cells = nx * ny * nz
    depth = rank // (2 * chips)
    lie = sketch.transpose(0, 1, 3, 2, 4).reshape(nx * ny, comps, nz, rank)
    snap = snapshots.transpose(0, 1, 3, 2, 4).reshape(nx * ny * comps, nz, snaps)
    extent = cells + 2 * ny * nz + 2 * nx * 16
    blocks = modes * modes // (2 * chips * 128)
    share = max(blocks // cols, 1)
    scale = 1.0 / math.sqrt(cells * 2 * chips * cols)
    counts = [4, 4, 1, 1] + [chips] * 2 + [cols] * 2 + [chips] * 4
    pieces = cols if blocks // cols else 1
    counts += [chips] * 4 + [cols] * 4 + [chips * pieces] * 4
    vmem = pl.BlockSpec(memory_space=pltpu.VMEM)
    return pl.pallas_call(
        functools.partial(kernel, chips, cols, nz, scale),
        out_shape=jax.ShapeDtypeStruct((modes, modes * modes), F32),
        in_specs=[pl.BlockSpec(memory_space=pltpu.HBM)] * 3,
        out_specs=vmem,
        scratch_shapes=[
            pltpu.VMEM(lie.shape, BF16),
            pltpu.VMEM(snap.shape, BF16),
            pltpu.VMEM((modes, rank), F32),
            pltpu.SemaphoreType.DMA((3,)),
            pltpu.VMEM((comps, nx, ny * nz, rank), BF16),
            pltpu.VMEM((2, rank // 2, comps * cells), BF16),
            pltpu.VMEM((2, comps, ny * nz, rank), BF16),
            pltpu.VMEM((2, comps, nx, 16, rank), BF16),
            pltpu.VMEM((chips, depth, snaps), F32),
            pltpu.VMEM((chips, depth, snaps), F32),
            pltpu.VMEM((chips, depth, snaps), F32),
            pltpu.VMEM((chips, depth, snaps), F32),
            pltpu.VMEM((cols, depth, snaps), F32),
            pltpu.VMEM((2, chips, depth, snaps), F32),
            pltpu.VMEM((extent, 3 * cells), BF16),
            pltpu.VMEM((comps, 2 * chips, modes // (2 * chips), cells), F32),
            pltpu.VMEM((modes, comps * cells), BF16),
            pltpu.VMEM((3, comps, modes, cells), BF16),
            pltpu.VMEM((blocks * 128, comps * cells), BF16),
            pltpu.VMEM((chips, blocks, modes, 128), BF16),
            pltpu.VMEM((chips, blocks, modes, 128), BF16),
            pltpu.VMEM((chips, blocks, modes, 128), BF16),
            pltpu.VMEM((chips, blocks, modes, 128), BF16),
            pltpu.VMEM((cols, share, modes, 128), BF16),
            pltpu.VMEM((cols, share, modes, 128), BF16),
            pltpu.VMEM((2, chips, blocks, modes, 128), BF16),
        ] + [pltpu.SemaphoreType.DMA((n,)) for n in counts],
        compiler_params=pltpu.CompilerParams(
            collective_id=0, has_side_effects=True, vmem_limit_bytes=40 * 1024 * 1024
        ),
    )(lie, snap, start_block.T)


def solution(mesh):
    chips, cols = mesh.shape["row"] // 2, mesh.shape["col"]
    return jax.shard_map(
        functools.partial(body, chips, cols),
        mesh=mesh,
        in_specs=(P("row", "col", None, None, None), P("row", "col", None, None, None), P()),
        out_specs=P(),
        check_vma=False,
    )
```

```python
import functools
import math

import jax
import jax.numpy as jnp
from jax import lax
from jax.experimental import pallas as pl
from jax.experimental.pallas import tpu as pltpu
from jax.sharding import PartitionSpec as P

ITERS = 4
MESH = pl.DeviceIdType.MESH
F32 = jnp.float32
BF16 = jnp.bfloat16
NT = (((1,), (1,)), ((), ()))


def neighbour_columns(nx, ny, nz):
    plane = ny * nz
    cells = nx * plane
    slab = 16
    cell = lax.broadcasted_iota(jnp.int32, (1, cells), 1)
    x, y, z = cell // plane, lax.rem(cell // nz, ny), lax.rem(cell, nz)
    x_before, x_after = cells, cells + plane
    y_before = cells + 2 * plane
    y_after = y_before + nx * slab
    ahead = [
        jnp.where(x < nx - 1, cell + plane, x_after + y * nz + z),
        jnp.where(y < ny - 1, cell + nz, y_after + x * slab + z),
        jnp.where(z < nz - 1, cell + 1, cell - (nz - 1)),
    ]
    behind = [
        jnp.where(x > 0, cell - plane, x_before + y * nz + z),
        jnp.where(y > 0, cell - nz, y_before + x * slab + slab - nz + z),
        jnp.where(z > 0, cell - 1, cell + nz - 1),
    ]
    return ahead, behind


def halves(value):
    high = value.astype(BF16)
    return high, (value - high.astype(F32)).astype(BF16)


def wide_left(value):
    high, low = halves(value)
    return jnp.concatenate([high, high, low], axis=1)


def kernel(
    chips, cols, span, scale,
    lie_hbm, snap_hbm, start_hbm, out_ref,
    lie_ref, snap_ref, start_ref, loads, sk_ref, sk_cols, hx, hy, sc1, rc1, acc1, rc2, rc3, cfull,
    diff, phi, phi_all, grad, adv,
    sg1, rg1, sg2, rg2, sg3, rg3, gfull,
    hs, hr, a1s, a1r, a2s, a2r, a3s, a3r, a4s, a4r, a5s, a5r,
    g1s, g1r, g2s, g2r, g3s, g3r, g4s, g4r, g5s, g5r, g6s, g6r,
):
    rows = 2 * chips
    row, col = lax.axis_index("row"), lax.axis_index("col")
    chip, core = row // 2, lax.rem(row, 2)
    sibling = (row + 1 - 2 * core, col)
    row_up, row_down = lax.rem(row + 1, rows), lax.rem(row + rows - 1, rows)
    col_up, col_down = lax.rem(col + 1, cols), lax.rem(col + cols - 1, cols)
    row_other = lax.rem(row + rows + 2 * core - 1, rows)

    def chip_at(offset):
        return lax.rem(chip + offset, chips)

    def col_at(offset):
        return lax.rem(col + offset, cols)

    def on_chip(q):
        return (2 * q + core, col)

    def push(src, dst, send, recv, device):
        return pltpu.make_async_remote_copy(
            src_ref=src, dst_ref=dst, send_sem=send, recv_sem=recv,
            device_id=device, device_id_type=MESH,
        )

    fetches = [
        pltpu.make_async_copy(src, dst, loads.at[n])
        for n, (src, dst) in enumerate(
            [(snap_hbm, snap_ref), (lie_hbm, lie_ref), (start_hbm, start_ref)]
        )
    ]
    for copy in fetches:
        copy.start()
    barrier = pltpu.get_barrier_semaphore()
    partners = [sibling, (row_other, col)]
    partners += [on_chip(chip_at(o)) for o in range(1, chips)]
    partners += [(row, col_at(o)) for o in range(1, cols)]
    for device in partners:
        pl.semaphore_signal(barrier, inc=1, device_id=device, device_id_type=MESH)

    comps, rank = sk_ref.shape[0], sk_ref.shape[-1]
    for copy in fetches:
        copy.wait()
    snaps = snap_ref[...].reshape(-1, snap_ref.shape[-1])
    sk_cols[...] = lie_ref[...].reshape(-1, rank).T.reshape(sk_cols.shape)
    for c in range(comps):
        sk_ref[c] = lie_ref[:, c].reshape(sk_ref.shape[1:])

    def projection(which):
        half = jnp.dot(sk_cols[which], snaps, preferred_element_type=F32)
        return half.reshape(sc1.shape)

    sc1[...] = projection(1 - core)
    pl.semaphore_wait(barrier, len(partners))
    a1 = push(sc1, rc1, a1s.at[0], a1r.at[0], sibling)
    a1.start()
    nx, plane = sk_ref.shape[1:3]
    halos = [
        push(sk_ref.at[:, nx - 1], hx.at[0], hs.at[0], hr.at[0], (row_up, col)),
        push(sk_ref.at[:, 0], hx.at[1], hs.at[1], hr.at[1], (row_down, col)),
        push(sk_ref.at[:, :, pl.ds(plane - 16, 16)], hy.at[0], hs.at[2], hr.at[2], (row, col_up)),
        push(sk_ref.at[:, :, pl.ds(0, 16)], hy.at[1], hs.at[3], hr.at[3], (row, col_down)),
    ]
    for copy in halos:
        copy.start()
    mine = projection(core)
    a1.wait_recv()
    acc1[...] = mine + rc1[...]
    a2 = []
    for o in range(1, chips):
        q = chip_at(o)
        copy = push(acc1.at[q], rc2.at[chip], a2s.at[o], a2r.at[chip], on_chip(q))
        copy.start()
        a2.append(copy)

    extent = diff.shape[0]
    cells = nx * plane
    place = lax.broadcasted_iota(jnp.int32, (extent, cells), 0)
    for d, (fore, aft) in enumerate(zip(*neighbour_columns(nx, plane // span, span))):
        diff[:, d * cells:(d + 1) * cells] = (
            jnp.where(place == fore, 0.5, 0.0) - jnp.where(place == aft, 0.5, 0.0)
        ).astype(BF16)

    total = acc1[chip]
    for o in range(1, chips):
        q = chip_at(o)
        push(rc2.at[q], rc2.at[q], a2s.at[o], a2r.at[q], sibling).wait_recv()
        total = total + rc2[q]
    rc3[col] = total
    a3 = []
    for o in range(1, cols):
        copy = push(rc3.at[col], rc3.at[col], a3s.at[o], a3r.at[col], (row, col_at(o)))
        copy.start()
        a3.append(copy)
    for o in range(1, cols):
        z = col_at(o)
        push(rc3.at[z], rc3.at[z], a3s.at[o], a3r.at[z], sibling).wait_recv()
    total = rc3[0]
    for z in range(1, cols):
        total = total + rc3[z]
    cfull[core, chip] = total
    own = cfull.at[core, chip]
    a5 = [push(own, own, a5s.at[0], a5r.at[chip], sibling)]
    a4 = []
    for o in range(1, chips):
        copy = push(own, own, a4s.at[o], a4r.at[chip], on_chip(chip_at(o)))
        copy.start()
        a4.append(copy)
    a5[0].start()
    for o in range(1, chips):
        q = chip_at(o)
        block = cfull.at[core, q]
        push(block, block, a4s.at[o], a4r.at[q], sibling).wait_recv()
        copy = push(block, block, a5s.at[o], a5r.at[q], sibling)
        copy.start()
        a5.append(copy)
    for q in range(chips):
        block = cfull.at[1 - core, q]
        push(block, block, a5s.at[0], a5r.at[q], sibling).wait_recv()

    coeffs = cfull[...].reshape(-1, cfull.shape[-1])
    start = start_ref[...]
    modes, rank = start.shape
    coeffs_h, coeffs_l = halves(coeffs)
    projected = jnp.dot(
        wide_left(start),
        jnp.concatenate([coeffs_h, coeffs_l, coeffs_h], axis=0),
        preferred_element_type=F32,
    )
    y_matrix = lax.dot_general(
        wide_left(projected),
        jnp.concatenate([coeffs_h, coeffs_l, coeffs_h], axis=1),
        NT, preferred_element_type=F32,
    )
    polar = y_matrix / jnp.sqrt(jnp.sum(y_matrix * y_matrix) + 1e-06)
    polar = jnp.concatenate([polar, jnp.zeros((-modes % 128, rank), F32)], axis=0)
    for _ in range(ITERS):
        high, low = halves(polar)
        gram = lax.dot_general(
            jnp.concatenate([high, high, low], axis=1),
            jnp.concatenate([high, low, high], axis=1),
            NT, preferred_element_type=F32,
        )
        polar = 1.5 * polar - 0.5 * jnp.dot(
            wide_left(gram),
            jnp.concatenate([high, low, high], axis=0),
            preferred_element_type=F32,
        )
    polar = polar[:modes]
    basis = polar.astype(BF16)

    for copy in halos:
        copy.wait_recv()
    for c in range(3):
        inner = sk_ref[c].reshape(cells, rank)
        outer = jnp.concatenate(
            [hx[0, c], hx[1, c], hy[0, c].reshape(-1, rank), hy[1, c].reshape(-1, rank)], axis=0
        )
        field = lax.dot_general(basis, inner, NT, preferred_element_type=F32).astype(BF16)
        rim = lax.dot_general(basis, outer, NT, preferred_element_type=F32).astype(BF16)
        phi[c] = field.astype(F32).reshape(phi.shape[1:])
        phi_all[:, c * cells:(c + 1) * cells] = field
        slopes = jnp.dot(
            jnp.concatenate([field, rim], axis=1), diff[...], preferred_element_type=F32
        ).astype(BF16)
        for d in range(3):
            grad[d, c] = slopes[:, d * cells:(d + 1) * cells]

    blocks = gfull.shape[2]
    count = 128 * blocks // modes

    def part(which, q):
        group_at = which * chips + q
        for ct in range(cells // 128):
            lanes = slice(ct * 128, ct * 128 + 128)
            for group in range(0, count, 4):
                some = range(group, min(group + 4, count))
                p = [
                    [
                        jnp.broadcast_to(phi[d, group_at, i:i + 1, lanes], (16, 128)).astype(BF16)
                        for d in range(3)
                    ]
                    for i in some
                ]
                for c in range(3):
                    for jt in range(0, modes, 16):
                        g = [grad[d, c, jt:jt + 16, lanes] for d in range(3)]
                        for i, pi in zip(some, p):
                            adv[
                                i * modes + jt:i * modes + jt + 16,
                                c * cells + ct * 128:c * cells + ct * 128 + 128,
                            ] = pi[0] * g[0] + pi[1] * g[1] + pi[2] * g[2]
        value = lax.dot_general(phi_all[...], adv[...], NT, preferred_element_type=F32)
        return [value[:, n * 128:n * 128 + 128] for n in range(blocks)]

    def theirs(step, carry):
        q = chip_at(step + 1)
        for n, value in enumerate(part(1 - core, q)):
            sg1[q, n] = value.astype(BF16)
        push(sg1.at[q], rg1.at[q], g1s.at[q], g1r.at[q], sibling).start()
        return carry

    lax.fori_loop(0, chips, theirs, 0)

    def ours(q):
        values = part(core, q)
        push(rg1.at[q], rg1.at[q], g1s.at[q], g1r.at[q], sibling).wait_recv()
        return [value + rg1[q, n].astype(F32) for n, value in enumerate(values)]

    def for_others(step, carry):
        q = chip_at(step + 1)
        for n, value in enumerate(ours(q)):
            sg2[q, n] = value.astype(BF16)
        push(sg2.at[q], rg2.at[chip], g2s.at[q], g2r.at[chip], on_chip(q)).start()
        return carry

    lax.fori_loop(0, chips - 1, for_others, 0)
    sums = ours(chip)
    for o in range(1, chips):
        q = chip_at(o)
        push(rg2.at[q], rg2.at[q], g2s.at[q], g2r.at[q], sibling).wait_recv()
        sums = [value + rg2[q, n].astype(F32) for n, value in enumerate(sums)]

    share = blocks // cols
    later = []
    if share:
        for n, value in enumerate(sums):
            sg3[n // share, n % share] = value.astype(BF16)
        for o in range(1, cols):
            z = col_at(o)
            copy = push(sg3.at[z], rg3.at[col], g3s.at[z], g3r.at[col], (row, z))
            copy.start()
            later.append(copy)
        final = sg3[col].astype(F32)
        for o in range(1, cols):
            z = col_at(o)
            push(rg3.at[z], rg3.at[z], g3s.at[z], g3r.at[z], sibling).wait_recv()
            final = final + rg3[z].astype(F32)
        gfull[core, chip, pl.ds(col * share, share)] = final.astype(BF16)
        own = gfull.at[core, chip, pl.ds(col * share, share)]
        for o in range(1, cols):
            z = col_at(o)
            copy = push(own, own, g4s.at[z], g4r.at[col], (row, z))
            copy.start()
            later.append(copy)
    else:
        for n, value in enumerate(sums):
            rg3[col, n] = value.astype(BF16)
        for o in range(1, cols):
            z = col_at(o)
            copy = push(rg3.at[col], rg3.at[col], g3s.at[z], g3r.at[col], (row, z))
            copy.start()
            later.append(copy)
        for o in range(1, cols):
            z = col_at(o)
            push(rg3.at[z], rg3.at[z], g3s.at[z], g3r.at[z], sibling).wait_recv()
        final = rg3[0].astype(F32)
        for z in range(1, cols):
            final = final + rg3[z].astype(F32)
        gfull[core, chip] = final.astype(BF16)

    pieces = cols if share else 1
    width = blocks // pieces

    def piece(which, q, z):
        return gfull.at[which, q, pl.ds(z * width, width)]

    def write(which, q, z):
        for n in range(width):
            block = z * width + n
            at = pl.multiple_of(((which * chips + q) * blocks + block) * 128, 128)
            out_ref[:, pl.ds(at, 128)] = gfull[which, q, block].astype(F32) * scale

    def forward(q, z):
        part_of = piece(core, q, z)
        copy = push(part_of, part_of, g6s.at[q * pieces + z], g6r.at[q * pieces + z], sibling)
        copy.start()
        later.append(copy)
        write(core, q, z)

    order = [col_at(o) for o in range(pieces)] if share else [0]
    for o, z in enumerate(order):
        own = piece(core, chip, z)
        if o:
            push(own, own, g4s.at[z], g4r.at[z], sibling).wait_recv()
        for offset in range(1, chips):
            q = chip_at(offset)
            copy = push(
                own, own, g5s.at[q * pieces + z], g5r.at[chip * pieces + z], on_chip(q)
            )
            copy.start()
            later.append(copy)
        forward(chip, z)
    for z in order:
        for offset in range(1, chips):
            q = chip_at(offset)
            block = piece(core, q, z)
            slot = q * pieces + z
            push(block, block, g5s.at[slot], g5r.at[slot], sibling).wait_recv()
            forward(q, z)
    for z in order:
        for offset in range(chips):
            q = chip_at(offset)
            block = piece(1 - core, q, z)
            slot = q * pieces + z
            push(block, block, g6s.at[slot], g6r.at[slot], sibling).wait_recv()
            write(1 - core, q, z)

    for copy in [a1, *halos, *a2, *a3, *a4, *a5, *later]:
        copy.wait_send()
    for q in range(chips):
        push(sg1.at[q], rg1.at[q], g1s.at[q], g1r.at[q], sibling).wait_send()
    for o in range(1, chips):
        q = chip_at(o)
        push(sg2.at[q], rg2.at[q], g2s.at[q], g2r.at[q], sibling).wait_send()


def body(chips, cols, sketch, snapshots, start_block):
    nx, ny, nz, comps, rank = sketch.shape
    snaps = snapshots.shape[-1]
    modes = start_block.shape[1]
    cells = nx * ny * nz
    depth = rank // (2 * chips)
    lie = sketch.transpose(0, 1, 3, 2, 4).reshape(nx * ny, comps, nz, rank)
    snap = snapshots.transpose(0, 1, 3, 2, 4).reshape(nx * ny * comps, nz, snaps)
    extent = cells + 2 * ny * nz + 2 * nx * 16
    blocks = modes * modes // (2 * chips * 128)
    share = max(blocks // cols, 1)
    scale = 1.0 / math.sqrt(cells * 2 * chips * cols)
    counts = [4, 4, 1, 1] + [chips] * 2 + [cols] * 2 + [chips] * 4
    pieces = cols if blocks // cols else 1
    counts += [chips] * 4 + [cols] * 4 + [chips * pieces] * 4
    vmem = pl.BlockSpec(memory_space=pltpu.VMEM)
    return pl.pallas_call(
        functools.partial(kernel, chips, cols, nz, scale),
        out_shape=jax.ShapeDtypeStruct((modes, modes * modes), F32),
        in_specs=[pl.BlockSpec(memory_space=pltpu.HBM)] * 3,
        out_specs=vmem,
        scratch_shapes=[
            pltpu.VMEM(lie.shape, BF16),
            pltpu.VMEM(snap.shape, BF16),
            pltpu.VMEM((modes, rank), F32),
            pltpu.SemaphoreType.DMA((3,)),
            pltpu.VMEM((comps, nx, ny * nz, rank), BF16),
            pltpu.VMEM((2, rank // 2, comps * cells), BF16),
            pltpu.VMEM((2, comps, ny * nz, rank), BF16),
            pltpu.VMEM((2, comps, nx, 16, rank), BF16),
            pltpu.VMEM((chips, depth, snaps), F32),
            pltpu.VMEM((chips, depth, snaps), F32),
            pltpu.VMEM((chips, depth, snaps), F32),
            pltpu.VMEM((chips, depth, snaps), F32),
            pltpu.VMEM((cols, depth, snaps), F32),
            pltpu.VMEM((2, chips, depth, snaps), F32),
            pltpu.VMEM((extent, 3 * cells), BF16),
            pltpu.VMEM((comps, 2 * chips, modes // (2 * chips), cells), F32),
            pltpu.VMEM((modes, comps * cells), BF16),
            pltpu.VMEM((3, comps, modes, cells), BF16),
            pltpu.VMEM((blocks * 128, comps * cells), BF16),
            pltpu.VMEM((chips, blocks, modes, 128), BF16),
            pltpu.VMEM((chips, blocks, modes, 128), BF16),
            pltpu.VMEM((chips, blocks, modes, 128), BF16),
            pltpu.VMEM((chips, blocks, modes, 128), BF16),
            pltpu.VMEM((cols, share, modes, 128), BF16),
            pltpu.VMEM((cols, share, modes, 128), BF16),
            pltpu.VMEM((2, chips, blocks, modes, 128), BF16),
        ] + [pltpu.SemaphoreType.DMA((n,)) for n in counts],
        compiler_params=pltpu.CompilerParams(
            collective_id=0, has_side_effects=True, vmem_limit_bytes=60 * 1024 * 1024
        ),
    )(lie, snap, start_block.T)


def solution(mesh):
    chips, cols = mesh.shape["row"] // 2, mesh.shape["col"]
    return jax.shard_map(
        functools.partial(body, chips, cols),
        mesh=mesh,
        in_specs=(P("row", "col", None, None, None), P("row", "col", None, None, None), P()),
        out_specs=P(),
        check_vma=False,
    )
```

```python
import functools
import math

import jax
import jax.numpy as jnp
from jax import lax
from jax.experimental import pallas as pl
from jax.experimental.pallas import tpu as pltpu
from jax.sharding import PartitionSpec as P

ITERS = 4
MESH = pl.DeviceIdType.MESH
F32 = jnp.float32
BF16 = jnp.bfloat16
NT = (((1,), (1,)), ((), ()))


def neighbour_columns(nx, ny, nz):
    plane = ny * nz
    cells = nx * plane
    slab = 16
    cell = lax.broadcasted_iota(jnp.int32, (1, cells), 1)
    x, y, z = cell // plane, lax.rem(cell // nz, ny), lax.rem(cell, nz)
    x_before, x_after = cells, cells + plane
    y_before = cells + 2 * plane
    y_after = y_before + nx * slab
    ahead = [
        jnp.where(x < nx - 1, cell + plane, x_after + y * nz + z),
        jnp.where(y < ny - 1, cell + nz, y_after + x * slab + z),
        jnp.where(z < nz - 1, cell + 1, cell - (nz - 1)),
    ]
    behind = [
        jnp.where(x > 0, cell - plane, x_before + y * nz + z),
        jnp.where(y > 0, cell - nz, y_before + x * slab + slab - nz + z),
        jnp.where(z > 0, cell - 1, cell + nz - 1),
    ]
    return ahead, behind


def halves(value):
    high = value.astype(BF16)
    return high, (value - high.astype(F32)).astype(BF16)


def wide_left(value):
    high, low = halves(value)
    return jnp.concatenate([high, high, low], axis=1)


def kernel(
    chips, cols, span,
    lie_hbm, snap_hbm, start_hbm, out_ref,
    lie_ref, snap_ref, start_ref, loads, stores, sk_ref, sk_cols, hx, hy, sc1, rc1, acc1, rc2, rc3, cfull,
    diff, phi, phi_all, grad, adv,
    sg1, rg1, sg2, rg2, sg3, rg3, gfull,
    hs, hr, a1s, a1r, a2s, a2r, a3s, a3r, a4s, a4r, a5s, a5r,
    g1s, g1r, g2s, g2r, g3s, g3r, g4s, g4r, g5s, g5r, g6s, g6r,
):
    rows = 2 * chips
    row, col = lax.axis_index("row"), lax.axis_index("col")
    chip, core = row // 2, lax.rem(row, 2)
    sibling = (row + 1 - 2 * core, col)
    row_up, row_down = lax.rem(row + 1, rows), lax.rem(row + rows - 1, rows)
    col_up, col_down = lax.rem(col + 1, cols), lax.rem(col + cols - 1, cols)
    row_other = lax.rem(row + rows + 2 * core - 1, rows)

    def chip_at(offset):
        return lax.rem(chip + offset, chips)

    def col_at(offset):
        return lax.rem(col + offset, cols)

    def on_chip(q):
        return (2 * q + core, col)

    def push(src, dst, send, recv, device):
        return pltpu.make_async_remote_copy(
            src_ref=src, dst_ref=dst, send_sem=send, recv_sem=recv,
            device_id=device, device_id_type=MESH,
        )

    fetches = [
        pltpu.make_async_copy(src, dst, loads.at[n])
        for n, (src, dst) in enumerate(
            [(snap_hbm, snap_ref), (lie_hbm, lie_ref), (start_hbm, start_ref)]
        )
    ]
    for copy in fetches:
        copy.start()
    barrier = pltpu.get_barrier_semaphore()
    partners = [sibling, (row_other, col)]
    partners += [on_chip(chip_at(o)) for o in range(1, chips)]
    partners += [(row, col_at(o)) for o in range(1, cols)]
    for device in partners:
        pl.semaphore_signal(barrier, inc=1, device_id=device, device_id_type=MESH)

    comps, rank = sk_ref.shape[0], sk_ref.shape[-1]
    for copy in fetches:
        copy.wait()
    snaps = snap_ref[...].reshape(-1, snap_ref.shape[-1])
    sk_cols[...] = lie_ref[...].reshape(-1, rank).T.reshape(sk_cols.shape)
    for c in range(comps):
        sk_ref[c] = lie_ref[:, c].reshape(sk_ref.shape[1:])

    def projection(which):
        half = jnp.dot(sk_cols[which], snaps, preferred_element_type=F32)
        return half.reshape(sc1.shape)

    sc1[...] = projection(1 - core)
    pl.semaphore_wait(barrier, len(partners))
    a1 = push(sc1, rc1, a1s.at[0], a1r.at[0], sibling)
    a1.start()
    nx, plane = sk_ref.shape[1:3]
    halos = [
        push(sk_ref.at[:, nx - 1], hx.at[0], hs.at[0], hr.at[0], (row_up, col)),
        push(sk_ref.at[:, 0], hx.at[1], hs.at[1], hr.at[1], (row_down, col)),
        push(sk_ref.at[:, :, pl.ds(plane - 16, 16)], hy.at[0], hs.at[2], hr.at[2], (row, col_up)),
        push(sk_ref.at[:, :, pl.ds(0, 16)], hy.at[1], hs.at[3], hr.at[3], (row, col_down)),
    ]
    for copy in halos:
        copy.start()
    mine = projection(core)
    a1.wait_recv()
    acc1[...] = mine + rc1[...]
    a2 = []
    for o in range(1, chips):
        q = chip_at(o)
        copy = push(acc1.at[q], rc2.at[chip], a2s.at[o], a2r.at[chip], on_chip(q))
        copy.start()
        a2.append(copy)

    extent = diff.shape[0]
    cells = nx * plane
    place = lax.broadcasted_iota(jnp.int32, (extent, cells), 0)
    for d, (fore, aft) in enumerate(zip(*neighbour_columns(nx, plane // span, span))):
        diff[:, d * cells:(d + 1) * cells] = (
            jnp.where(place == fore, 0.5, 0.0) - jnp.where(place == aft, 0.5, 0.0)
        ).astype(BF16)

    total = acc1[chip]
    for o in range(1, chips):
        q = chip_at(o)
        push(rc2.at[q], rc2.at[q], a2s.at[o], a2r.at[q], sibling).wait_recv()
        total = total + rc2[q]
    rc3[col] = total
    a3 = []
    for o in range(1, cols):
        copy = push(rc3.at[col], rc3.at[col], a3s.at[o], a3r.at[col], (row, col_at(o)))
        copy.start()
        a3.append(copy)
    for o in range(1, cols):
        z = col_at(o)
        push(rc3.at[z], rc3.at[z], a3s.at[o], a3r.at[z], sibling).wait_recv()
    total = rc3[0]
    for z in range(1, cols):
        total = total + rc3[z]
    cfull[core, chip] = total
    own = cfull.at[core, chip]
    a5 = [push(own, own, a5s.at[0], a5r.at[chip], sibling)]
    a4 = []
    for o in range(1, chips):
        copy = push(own, own, a4s.at[o], a4r.at[chip], on_chip(chip_at(o)))
        copy.start()
        a4.append(copy)
    a5[0].start()
    for o in range(1, chips):
        q = chip_at(o)
        block = cfull.at[core, q]
        push(block, block, a4s.at[o], a4r.at[q], sibling).wait_recv()
        copy = push(block, block, a5s.at[o], a5r.at[q], sibling)
        copy.start()
        a5.append(copy)
    for q in range(chips):
        block = cfull.at[1 - core, q]
        push(block, block, a5s.at[0], a5r.at[q], sibling).wait_recv()

    coeffs = cfull[...].reshape(-1, cfull.shape[-1])
    start = start_ref[...]
    modes, rank = start.shape
    coeffs_h, coeffs_l = halves(coeffs)
    projected = jnp.dot(
        wide_left(start),
        jnp.concatenate([coeffs_h, coeffs_l, coeffs_h], axis=0),
        preferred_element_type=F32,
    )
    y_matrix = lax.dot_general(
        wide_left(projected),
        jnp.concatenate([coeffs_h, coeffs_l, coeffs_h], axis=1),
        NT, preferred_element_type=F32,
    )
    polar = y_matrix / jnp.sqrt(jnp.sum(y_matrix * y_matrix) + 1e-06)
    polar = jnp.concatenate([polar, jnp.zeros((-modes % 128, rank), F32)], axis=0)
    for _ in range(ITERS):
        high, low = halves(polar)
        gram = lax.dot_general(
            jnp.concatenate([high, high, low], axis=1),
            jnp.concatenate([high, low, high], axis=1),
            NT, preferred_element_type=F32,
        )
        polar = 1.5 * polar - 0.5 * jnp.dot(
            wide_left(gram),
            jnp.concatenate([high, low, high], axis=0),
            preferred_element_type=F32,
        )
    polar = polar[:modes]
    basis = polar.astype(BF16)

    for copy in halos:
        copy.wait_recv()
    for c in range(3):
        inner = sk_ref[c].reshape(cells, rank)
        outer = jnp.concatenate(
            [hx[0, c], hx[1, c], hy[0, c].reshape(-1, rank), hy[1, c].reshape(-1, rank)], axis=0
        )
        field = lax.dot_general(basis, inner, NT, preferred_element_type=F32).astype(BF16)
        rim = lax.dot_general(basis, outer, NT, preferred_element_type=F32).astype(BF16)
        phi[c] = field.astype(F32).reshape(phi.shape[1:])
        phi_all[c * cells:(c + 1) * cells] = lax.dot_general(
            inner, basis, NT, preferred_element_type=F32
        ).astype(BF16)
        slopes = jnp.dot(
            jnp.concatenate([field, rim], axis=1), diff[...], preferred_element_type=F32
        ).astype(BF16)
        for d in range(3):
            grad[d, c] = slopes[:, d * cells:(d + 1) * cells]

    blocks = gfull.shape[2]
    count = 128 * blocks // modes

    def part(which, q):
        group_at = which * chips + q
        for ct in range(cells // 128):
            lanes = slice(ct * 128, ct * 128 + 128)
            for group in range(0, count, 4):
                some = range(group, min(group + 4, count))
                p = [
                    [
                        jnp.broadcast_to(phi[d, group_at, i:i + 1, lanes], (16, 128)).astype(BF16)
                        for d in range(3)
                    ]
                    for i in some
                ]
                for c in range(3):
                    for jt in range(0, modes, 16):
                        g = [grad[d, c, jt:jt + 16, lanes] for d in range(3)]
                        for i, pi in zip(some, p):
                            adv[
                                i * modes + jt:i * modes + jt + 16,
                                c * cells + ct * 128:c * cells + ct * 128 + 128,
                            ] = pi[0] * g[0] + pi[1] * g[1] + pi[2] * g[2]
        value = jnp.dot(adv[...], phi_all[...], preferred_element_type=F32)
        return [value[n * 128:n * 128 + 128].T for n in range(blocks)]

    def theirs(step, carry):
        q = chip_at(step + 1)
        for n, value in enumerate(part(1 - core, q)):
            sg1[q, n] = value.astype(BF16)
        push(sg1.at[q], rg1.at[q], g1s.at[q], g1r.at[q], sibling).start()
        return carry

    lax.fori_loop(0, chips, theirs, 0)

    def ours(q):
        values = part(core, q)
        push(rg1.at[q], rg1.at[q], g1s.at[q], g1r.at[q], sibling).wait_recv()
        return [value + rg1[q, n].astype(F32) for n, value in enumerate(values)]

    def for_others(step, carry):
        q = chip_at(step + 1)
        for n, value in enumerate(ours(q)):
            sg2[q, n] = value.astype(BF16)
        push(sg2.at[q], rg2.at[chip], g2s.at[q], g2r.at[chip], on_chip(q)).start()
        return carry

    lax.fori_loop(0, chips - 1, for_others, 0)
    sums = ours(chip)
    for o in range(1, chips):
        q = chip_at(o)
        push(rg2.at[q], rg2.at[q], g2s.at[q], g2r.at[q], sibling).wait_recv()
        sums = [value + rg2[q, n].astype(F32) for n, value in enumerate(sums)]

    share = blocks // cols
    later = []
    if share:
        for n, value in enumerate(sums):
            sg3[n // share, n % share] = value.astype(BF16)
        for o in range(1, cols):
            z = col_at(o)
            copy = push(sg3.at[z], rg3.at[col], g3s.at[z], g3r.at[col], (row, z))
            copy.start()
            later.append(copy)
        final = sg3[col].astype(F32)
        for o in range(1, cols):
            z = col_at(o)
            push(rg3.at[z], rg3.at[z], g3s.at[z], g3r.at[z], sibling).wait_recv()
            final = final + rg3[z].astype(F32)
        gfull[core, chip, pl.ds(col * share, share)] = final.astype(BF16)
        own = gfull.at[core, chip, pl.ds(col * share, share)]
        for o in range(1, cols):
            z = col_at(o)
            copy = push(own, own, g4s.at[z], g4r.at[col], (row, z))
            copy.start()
            later.append(copy)
    else:
        for n, value in enumerate(sums):
            rg3[col, n] = value.astype(BF16)
        for o in range(1, cols):
            z = col_at(o)
            copy = push(rg3.at[col], rg3.at[col], g3s.at[z], g3r.at[col], (row, z))
            copy.start()
            later.append(copy)
        for o in range(1, cols):
            z = col_at(o)
            push(rg3.at[z], rg3.at[z], g3s.at[z], g3r.at[z], sibling).wait_recv()
        final = rg3[0].astype(F32)
        for z in range(1, cols):
            final = final + rg3[z].astype(F32)
        gfull[core, chip] = final.astype(BF16)

    pieces = cols if share else 1
    width = blocks // pieces

    def piece(which, q, z):
        return gfull.at[which, q, pl.ds(z * width, width)]

    outs = []

    def write(which, q, z):
        slot = (which * chips + q) * pieces + z
        copy = pltpu.make_async_copy(
            piece(which, q, z), out_ref.at[pl.ds(slot * width, width)], stores.at[slot]
        )
        copy.start()
        outs.append(copy)

    def forward(q, z):
        part_of = piece(core, q, z)
        copy = push(part_of, part_of, g6s.at[q * pieces + z], g6r.at[q * pieces + z], sibling)
        copy.start()
        later.append(copy)
        write(core, q, z)

    order = [col_at(o) for o in range(pieces)] if share else [0]
    for o, z in enumerate(order):
        own = piece(core, chip, z)
        if o:
            push(own, own, g4s.at[z], g4r.at[z], sibling).wait_recv()
        for offset in range(1, chips):
            q = chip_at(offset)
            copy = push(
                own, own, g5s.at[q * pieces + z], g5r.at[chip * pieces + z], on_chip(q)
            )
            copy.start()
            later.append(copy)
        forward(chip, z)
    for z in order:
        for offset in range(1, chips):
            q = chip_at(offset)
            block = piece(core, q, z)
            slot = q * pieces + z
            push(block, block, g5s.at[slot], g5r.at[slot], sibling).wait_recv()
            forward(q, z)
    for z in order:
        for offset in range(chips):
            q = chip_at(offset)
            block = piece(1 - core, q, z)
            slot = q * pieces + z
            push(block, block, g6s.at[slot], g6r.at[slot], sibling).wait_recv()
            write(1 - core, q, z)

    for copy in outs:
        copy.wait()
    for copy in [a1, *halos, *a2, *a3, *a4, *a5, *later]:
        copy.wait_send()
    for q in range(chips):
        push(sg1.at[q], rg1.at[q], g1s.at[q], g1r.at[q], sibling).wait_send()
    for o in range(1, chips):
        q = chip_at(o)
        push(sg2.at[q], rg2.at[q], g2s.at[q], g2r.at[q], sibling).wait_send()


def body(chips, cols, sketch, snapshots, start_block):
    nx, ny, nz, comps, rank = sketch.shape
    snaps = snapshots.shape[-1]
    modes = start_block.shape[1]
    cells = nx * ny * nz
    depth = rank // (2 * chips)
    lie = sketch.transpose(0, 1, 3, 2, 4).reshape(nx * ny, comps, nz, rank)
    snap = snapshots.transpose(0, 1, 3, 2, 4).reshape(nx * ny * comps, nz, snaps)
    extent = cells + 2 * ny * nz + 2 * nx * 16
    blocks = modes * modes // (2 * chips * 128)
    share = max(blocks // cols, 1)
    scale = 1.0 / math.sqrt(cells * 2 * chips * cols)
    counts = [4, 4, 1, 1] + [chips] * 2 + [cols] * 2 + [chips] * 4
    pieces = cols if blocks // cols else 1
    counts += [chips] * 4 + [cols] * 4 + [chips * pieces] * 4
    tensor = pl.pallas_call(
        functools.partial(kernel, chips, cols, nz),
        out_shape=jax.ShapeDtypeStruct((2 * chips * blocks, modes, 128), BF16),
        in_specs=[pl.BlockSpec(memory_space=pltpu.HBM)] * 3,
        out_specs=pl.BlockSpec(memory_space=pltpu.HBM),
        scratch_shapes=[
            pltpu.VMEM(lie.shape, BF16),
            pltpu.VMEM(snap.shape, BF16),
            pltpu.VMEM((modes, rank), F32),
            pltpu.SemaphoreType.DMA((3,)),
            pltpu.SemaphoreType.DMA((2 * chips * pieces,)),
            pltpu.VMEM((comps, nx, ny * nz, rank), BF16),
            pltpu.VMEM((2, rank // 2, comps * cells), BF16),
            pltpu.VMEM((2, comps, ny * nz, rank), BF16),
            pltpu.VMEM((2, comps, nx, 16, rank), BF16),
            pltpu.VMEM((chips, depth, snaps), F32),
            pltpu.VMEM((chips, depth, snaps), F32),
            pltpu.VMEM((chips, depth, snaps), F32),
            pltpu.VMEM((chips, depth, snaps), F32),
            pltpu.VMEM((cols, depth, snaps), F32),
            pltpu.VMEM((2, chips, depth, snaps), F32),
            pltpu.VMEM((extent, 3 * cells), BF16),
            pltpu.VMEM((comps, 2 * chips, modes // (2 * chips), cells), F32),
            pltpu.VMEM((comps * cells, modes), BF16),
            pltpu.VMEM((3, comps, modes, cells), BF16),
            pltpu.VMEM((blocks * 128, comps * cells), BF16),
            pltpu.VMEM((chips, blocks, modes, 128), BF16),
            pltpu.VMEM((chips, blocks, modes, 128), BF16),
            pltpu.VMEM((chips, blocks, modes, 128), BF16),
            pltpu.VMEM((chips, blocks, modes, 128), BF16),
            pltpu.VMEM((cols, share, modes, 128), BF16),
            pltpu.VMEM((cols, share, modes, 128), BF16),
            pltpu.VMEM((2, chips, blocks, modes, 128), BF16),
        ] + [pltpu.SemaphoreType.DMA((n,)) for n in counts],
        compiler_params=pltpu.CompilerParams(
            collective_id=0, has_side_effects=True, vmem_limit_bytes=60 * 1024 * 1024
        ),
    )(lie, snap, start_block.T)
    tensor = (tensor.astype(F32) * scale).transpose(1, 0, 2)
    return tensor.reshape(modes, modes * modes)


def solution(mesh):
    chips, cols = mesh.shape["row"] // 2, mesh.shape["col"]
    return jax.shard_map(
        functools.partial(body, chips, cols),
        mesh=mesh,
        in_specs=(P("row", "col", None, None, None), P("row", "col", None, None, None), P()),
        out_specs=P(),
        check_vma=False,
    )
```

```python
import functools
import math

import jax
import jax.numpy as jnp
from jax import lax
from jax.experimental import pallas as pl
from jax.experimental.pallas import tpu as pltpu
from jax.sharding import PartitionSpec as P

ITERS = 4
MESH = pl.DeviceIdType.MESH
F32 = jnp.float32
BF16 = jnp.bfloat16
NT = (((1,), (1,)), ((), ()))


def neighbour_columns(nx, ny, nz):
    plane = ny * nz
    cells = nx * plane
    slab = 16
    cell = lax.broadcasted_iota(jnp.int32, (1, cells), 1)
    x, y, z = cell // plane, lax.rem(cell // nz, ny), lax.rem(cell, nz)
    x_before, x_after = cells, cells + plane
    y_before = cells + 2 * plane
    y_after = y_before + nx * slab
    ahead = [
        jnp.where(x < nx - 1, cell + plane, x_after + y * nz + z),
        jnp.where(y < ny - 1, cell + nz, y_after + x * slab + z),
        jnp.where(z < nz - 1, cell + 1, cell - (nz - 1)),
    ]
    behind = [
        jnp.where(x > 0, cell - plane, x_before + y * nz + z),
        jnp.where(y > 0, cell - nz, y_before + x * slab + slab - nz + z),
        jnp.where(z > 0, cell - 1, cell + nz - 1),
    ]
    return ahead, behind


def halves(value):
    high = value.astype(BF16)
    return high, (value - high.astype(F32)).astype(BF16)


def wide_left(value):
    high, low = halves(value)
    return jnp.concatenate([high, high, low], axis=1)


def kernel(
    chips, cols, span,
    lie_hbm, snap_hbm, start_hbm, out_ref,
    lie_ref, snap_ref, start_ref, loads, stores, sk_ref, sk_cols, hx, hy, sc1, rc1, acc1, rc2, rc3, cfull,
    diff, phi, phi_all, grad, adv,
    sg1, rg1, sg2, rg2, sg3, rg3, gfull,
    hs, hr, a1s, a1r, a2s, a2r, a3s, a3r, a4s, a4r, a5s, a5r,
    g1s, g1r, g2s, g2r, g3s, g3r, g4s, g4r, g5s, g5r, g6s, g6r,
):
    rows = 2 * chips
    row, col = lax.axis_index("row"), lax.axis_index("col")
    chip, core = row // 2, lax.rem(row, 2)
    sibling = (row + 1 - 2 * core, col)
    row_up, row_down = lax.rem(row + 1, rows), lax.rem(row + rows - 1, rows)
    col_up, col_down = lax.rem(col + 1, cols), lax.rem(col + cols - 1, cols)
    row_other = lax.rem(row + rows + 2 * core - 1, rows)

    def chip_at(offset):
        return lax.rem(chip + offset, chips)

    def col_at(offset):
        return lax.rem(col + offset, cols)

    def on_chip(q):
        return (2 * q + core, col)

    def push(src, dst, send, recv, device):
        return pltpu.make_async_remote_copy(
            src_ref=src, dst_ref=dst, send_sem=send, recv_sem=recv,
            device_id=device, device_id_type=MESH,
        )

    fetches = [
        pltpu.make_async_copy(src, dst, loads.at[n])
        for n, (src, dst) in enumerate(
            [(snap_hbm, snap_ref), (lie_hbm, lie_ref), (start_hbm, start_ref)]
        )
    ]
    for copy in fetches:
        copy.start()
    barrier = pltpu.get_barrier_semaphore()
    partners = [sibling, (row_other, col)]
    partners += [on_chip(chip_at(o)) for o in range(1, chips)]
    partners += [(row, col_at(o)) for o in range(1, cols)]
    for device in partners:
        pl.semaphore_signal(barrier, inc=1, device_id=device, device_id_type=MESH)

    comps, rank = sk_ref.shape[0], sk_ref.shape[-1]
    for copy in fetches:
        copy.wait()
    snaps = snap_ref[...].reshape(-1, snap_ref.shape[-1])
    sk_cols[...] = lie_ref[...].reshape(-1, rank).T.reshape(sk_cols.shape)
    for c in range(comps):
        sk_ref[c] = lie_ref[:, c].reshape(sk_ref.shape[1:])

    waves = range(sc1.shape[0])

    def projection(which):
        half = jnp.dot(sk_cols[which], snaps, preferred_element_type=F32)
        size = sc1.shape[-1]
        return [half[:, w * size:(w + 1) * size].reshape(sc1.shape[1:]) for w in waves]

    for w, value in enumerate(projection(1 - core)):
        sc1[w] = value
    pl.semaphore_wait(barrier, len(partners))
    a1 = [push(sc1.at[w], rc1.at[w], a1s.at[w], a1r.at[w], sibling) for w in waves]
    for copy in a1:
        copy.start()
    nx, plane = sk_ref.shape[1:3]
    halos = [
        push(sk_ref.at[:, nx - 1], hx.at[0], hs.at[0], hr.at[0], (row_up, col)),
        push(sk_ref.at[:, 0], hx.at[1], hs.at[1], hr.at[1], (row_down, col)),
        push(sk_ref.at[:, :, pl.ds(plane - 16, 16)], hy.at[0], hs.at[2], hr.at[2], (row, col_up)),
        push(sk_ref.at[:, :, pl.ds(0, 16)], hy.at[1], hs.at[3], hr.at[3], (row, col_down)),
    ]
    for copy in halos:
        copy.start()
    mine = projection(core)
    a2 = []
    for w in waves:
        a1[w].wait_recv()
        acc1[w] = mine[w] + rc1[w]
        for o in range(1, chips):
            q = chip_at(o)
            copy = push(
                acc1.at[w, q], rc2.at[w, chip],
                a2s.at[w * chips + o], a2r.at[w * chips + chip], on_chip(q),
            )
            copy.start()
            a2.append(copy)

    extent = diff.shape[0]
    cells = nx * plane
    place = lax.broadcasted_iota(jnp.int32, (extent, cells), 0)
    for d, (fore, aft) in enumerate(zip(*neighbour_columns(nx, plane // span, span))):
        diff[:, d * cells:(d + 1) * cells] = (
            jnp.where(place == fore, 0.5, 0.0) - jnp.where(place == aft, 0.5, 0.0)
        ).astype(BF16)

    a3 = []
    for w in waves:
        total = acc1[w, chip]
        for o in range(1, chips):
            q = chip_at(o)
            block = rc2.at[w, q]
            push(block, block, a2s.at[0], a2r.at[w * chips + q], sibling).wait_recv()
            total = total + rc2[w, q]
        rc3[w, col] = total
        own = rc3.at[w, col]
        for o in range(1, cols):
            copy = push(
                own, own, a3s.at[w * cols + o], a3r.at[w * cols + col], (row, col_at(o))
            )
            copy.start()
            a3.append(copy)
    a4, a5 = [], []
    for w in waves:
        for o in range(1, cols):
            z = col_at(o)
            block = rc3.at[w, z]
            push(block, block, a3s.at[0], a3r.at[w * cols + z], sibling).wait_recv()
        total = rc3[w, 0]
        for z in range(1, cols):
            total = total + rc3[w, z]
        cfull[w, core, chip] = total
        own = cfull.at[w, core, chip]
        for o in range(1, chips):
            copy = push(
                own, own, a4s.at[w * chips + o], a4r.at[w * chips + chip], on_chip(chip_at(o))
            )
            copy.start()
            a4.append(copy)
        copy = push(own, own, a5s.at[w * chips], a5r.at[w * chips + chip], sibling)
        copy.start()
        a5.append(copy)
    for w in waves:
        for o in range(1, chips):
            q = chip_at(o)
            block = cfull.at[w, core, q]
            push(block, block, a4s.at[0], a4r.at[w * chips + q], sibling).wait_recv()
            copy = push(block, block, a5s.at[w * chips + o], a5r.at[w * chips + q], sibling)
            copy.start()
            a5.append(copy)
    for w in waves:
        for q in range(chips):
            block = cfull.at[w, 1 - core, q]
            push(block, block, a5s.at[0], a5r.at[w * chips + q], sibling).wait_recv()

    coeffs = jnp.concatenate([cfull[w].reshape(rank, -1) for w in waves], axis=1)
    start = start_ref[...]
    modes, rank = start.shape
    coeffs_h, coeffs_l = halves(coeffs)
    projected = jnp.dot(
        wide_left(start),
        jnp.concatenate([coeffs_h, coeffs_l, coeffs_h], axis=0),
        preferred_element_type=F32,
    )
    y_matrix = lax.dot_general(
        wide_left(projected),
        jnp.concatenate([coeffs_h, coeffs_l, coeffs_h], axis=1),
        NT, preferred_element_type=F32,
    )
    polar = y_matrix / jnp.sqrt(jnp.sum(y_matrix * y_matrix) + 1e-06)
    polar = jnp.concatenate([polar, jnp.zeros((-modes % 128, rank), F32)], axis=0)
    for _ in range(ITERS):
        high, low = halves(polar)
        gram = lax.dot_general(
            jnp.concatenate([high, high, low], axis=1),
            jnp.concatenate([high, low, high], axis=1),
            NT, preferred_element_type=F32,
        )
        polar = 1.5 * polar - 0.5 * jnp.dot(
            wide_left(gram),
            jnp.concatenate([high, low, high], axis=0),
            preferred_element_type=F32,
        )
    polar = polar[:modes]
    basis = polar.astype(BF16)

    for copy in halos:
        copy.wait_recv()
    for c in range(3):
        inner = sk_ref[c].reshape(cells, rank)
        outer = jnp.concatenate(
            [hx[0, c], hx[1, c], hy[0, c].reshape(-1, rank), hy[1, c].reshape(-1, rank)], axis=0
        )
        field = lax.dot_general(basis, inner, NT, preferred_element_type=F32).astype(BF16)
        rim = lax.dot_general(basis, outer, NT, preferred_element_type=F32).astype(BF16)
        phi[c] = field.astype(F32).reshape(phi.shape[1:])
        phi_all[c * cells:(c + 1) * cells] = lax.dot_general(
            inner, basis, NT, preferred_element_type=F32
        ).astype(BF16)
        slopes = jnp.dot(
            jnp.concatenate([field, rim], axis=1), diff[...], preferred_element_type=F32
        ).astype(BF16)
        for d in range(3):
            grad[d, c] = slopes[:, d * cells:(d + 1) * cells]

    blocks = gfull.shape[2]
    count = 128 * blocks // modes

    def part(which, q):
        group_at = which * chips + q
        for ct in range(cells // 128):
            lanes = slice(ct * 128, ct * 128 + 128)
            for group in range(0, count, 4):
                some = range(group, min(group + 4, count))
                p = [
                    [
                        jnp.broadcast_to(phi[d, group_at, i:i + 1, lanes], (16, 128)).astype(BF16)
                        for d in range(3)
                    ]
                    for i in some
                ]
                for c in range(3):
                    for jt in range(0, modes, 16):
                        g = [grad[d, c, jt:jt + 16, lanes] for d in range(3)]
                        for i, pi in zip(some, p):
                            adv[
                                i * modes + jt:i * modes + jt + 16,
                                c * cells + ct * 128:c * cells + ct * 128 + 128,
                            ] = pi[0] * g[0] + pi[1] * g[1] + pi[2] * g[2]
        value = jnp.dot(adv[...], phi_all[...], preferred_element_type=F32)
        return [value[n * 128:n * 128 + 128].T for n in range(blocks)]

    def theirs(step, carry):
        q = chip_at(step + 1)
        for n, value in enumerate(part(1 - core, q)):
            sg1[q, n] = value.astype(BF16)
        push(sg1.at[q], rg1.at[q], g1s.at[q], g1r.at[q], sibling).start()
        return carry

    lax.fori_loop(0, chips, theirs, 0)

    def ours(q):
        values = part(core, q)
        push(rg1.at[q], rg1.at[q], g1s.at[q], g1r.at[q], sibling).wait_recv()
        return [value + rg1[q, n].astype(F32) for n, value in enumerate(values)]

    def for_others(step, carry):
        q = chip_at(step + 1)
        for n, value in enumerate(ours(q)):
            sg2[q, n] = value.astype(BF16)
        push(sg2.at[q], rg2.at[chip], g2s.at[q], g2r.at[chip], on_chip(q)).start()
        return carry

    lax.fori_loop(0, chips - 1, for_others, 0)
    sums = ours(chip)
    for o in range(1, chips):
        q = chip_at(o)
        push(rg2.at[q], rg2.at[q], g2s.at[q], g2r.at[q], sibling).wait_recv()
        sums = [value + rg2[q, n].astype(F32) for n, value in enumerate(sums)]

    share = blocks // cols
    later = []
    if share:
        for n, value in enumerate(sums):
            sg3[n // share, n % share] = value.astype(BF16)
        for o in range(1, cols):
            z = col_at(o)
            copy = push(sg3.at[z], rg3.at[col], g3s.at[z], g3r.at[col], (row, z))
            copy.start()
            later.append(copy)
        final = sg3[col].astype(F32)
        for o in range(1, cols):
            z = col_at(o)
            push(rg3.at[z], rg3.at[z], g3s.at[z], g3r.at[z], sibling).wait_recv()
            final = final + rg3[z].astype(F32)
        gfull[core, chip, pl.ds(col * share, share)] = final.astype(BF16)
        own = gfull.at[core, chip, pl.ds(col * share, share)]
        for o in range(1, cols):
            z = col_at(o)
            copy = push(own, own, g4s.at[z], g4r.at[col], (row, z))
            copy.start()
            later.append(copy)
    else:
        for n, value in enumerate(sums):
            rg3[col, n] = value.astype(BF16)
        for o in range(1, cols):
            z = col_at(o)
            copy = push(rg3.at[col], rg3.at[col], g3s.at[z], g3r.at[col], (row, z))
            copy.start()
            later.append(copy)
        for o in range(1, cols):
            z = col_at(o)
            push(rg3.at[z], rg3.at[z], g3s.at[z], g3r.at[z], sibling).wait_recv()
        final = rg3[0].astype(F32)
        for z in range(1, cols):
            final = final + rg3[z].astype(F32)
        gfull[core, chip] = final.astype(BF16)

    pieces = cols if share else 1
    width = blocks // pieces

    def piece(which, q, z):
        return gfull.at[which, q, pl.ds(z * width, width)]

    outs = []

    def write(which, q, z):
        slot = (which * chips + q) * pieces + z
        copy = pltpu.make_async_copy(
            piece(which, q, z), out_ref.at[pl.ds(slot * width, width)], stores.at[slot]
        )
        copy.start()
        outs.append(copy)

    def forward(q, z):
        part_of = piece(core, q, z)
        copy = push(part_of, part_of, g6s.at[q * pieces + z], g6r.at[q * pieces + z], sibling)
        copy.start()
        later.append(copy)
        write(core, q, z)

    order = [col_at(o) for o in range(pieces)] if share else [0]
    for o, z in enumerate(order):
        own = piece(core, chip, z)
        if o:
            push(own, own, g4s.at[z], g4r.at[z], sibling).wait_recv()
        for offset in range(1, chips):
            q = chip_at(offset)
            copy = push(
                own, own, g5s.at[q * pieces + z], g5r.at[chip * pieces + z], on_chip(q)
            )
            copy.start()
            later.append(copy)
        forward(chip, z)
    for z in order:
        for offset in range(1, chips):
            q = chip_at(offset)
            block = piece(core, q, z)
            slot = q * pieces + z
            push(block, block, g5s.at[slot], g5r.at[slot], sibling).wait_recv()
            forward(q, z)
    for z in order:
        for offset in range(chips):
            q = chip_at(offset)
            block = piece(1 - core, q, z)
            slot = q * pieces + z
            push(block, block, g6s.at[slot], g6r.at[slot], sibling).wait_recv()
            write(1 - core, q, z)

    for copy in outs:
        copy.wait()
    for copy in [*a1, *halos, *a2, *a3, *a4, *a5, *later]:
        copy.wait_send()
    for q in range(chips):
        push(sg1.at[q], rg1.at[q], g1s.at[q], g1r.at[q], sibling).wait_send()
    for o in range(1, chips):
        q = chip_at(o)
        push(sg2.at[q], rg2.at[q], g2s.at[q], g2r.at[q], sibling).wait_send()


def widen(scale, pieces_ref, out_ref):
    for n in range(pieces_ref.shape[0]):
        out_ref[:, n * 128:n * 128 + 128] = pieces_ref[n].astype(F32) * scale


def body(chips, cols, sketch, snapshots, start_block):
    nx, ny, nz, comps, rank = sketch.shape
    snaps = snapshots.shape[-1]
    modes = start_block.shape[1]
    cells = nx * ny * nz
    depth = rank // (2 * chips)
    lie = sketch.transpose(0, 1, 3, 2, 4).reshape(nx * ny, comps, nz, rank)
    snap = snapshots.transpose(0, 1, 3, 2, 4).reshape(nx * ny * comps, nz, snaps)
    extent = cells + 2 * ny * nz + 2 * nx * 16
    blocks = modes * modes // (2 * chips * 128)
    share = max(blocks // cols, 1)
    scale = 1.0 / math.sqrt(cells * 2 * chips * cols)
    waves = 2
    counts = [4, 4, waves, waves] + [waves * chips] * 2 + [waves * cols] * 2
    counts += [waves * chips] * 4
    pieces = cols if blocks // cols else 1
    counts += [chips] * 4 + [cols] * 4 + [chips * pieces] * 4
    tensor = pl.pallas_call(
        functools.partial(kernel, chips, cols, nz),
        out_shape=jax.ShapeDtypeStruct((2 * chips * blocks, modes, 128), BF16),
        in_specs=[pl.BlockSpec(memory_space=pltpu.HBM)] * 3,
        out_specs=pl.BlockSpec(memory_space=pltpu.HBM),
        scratch_shapes=[
            pltpu.VMEM(lie.shape, BF16),
            pltpu.VMEM(snap.shape, BF16),
            pltpu.VMEM((modes, rank), F32),
            pltpu.SemaphoreType.DMA((3,)),
            pltpu.SemaphoreType.DMA((2 * chips * pieces,)),
            pltpu.VMEM((comps, nx, ny * nz, rank), BF16),
            pltpu.VMEM((2, rank // 2, comps * cells), BF16),
            pltpu.VMEM((2, comps, ny * nz, rank), BF16),
            pltpu.VMEM((2, comps, nx, 16, rank), BF16),
            pltpu.VMEM((waves, chips, depth, snaps // waves), F32),
            pltpu.VMEM((waves, chips, depth, snaps // waves), F32),
            pltpu.VMEM((waves, chips, depth, snaps // waves), F32),
            pltpu.VMEM((waves, chips, depth, snaps // waves), F32),
            pltpu.VMEM((waves, cols, depth, snaps // waves), F32),
            pltpu.VMEM((waves, 2, chips, depth, snaps // waves), F32),
            pltpu.VMEM((extent, 3 * cells), BF16),
            pltpu.VMEM((comps, 2 * chips, modes // (2 * chips), cells), F32),
            pltpu.VMEM((comps * cells, modes), BF16),
            pltpu.VMEM((3, comps, modes, cells), BF16),
            pltpu.VMEM((blocks * 128, comps * cells), BF16),
            pltpu.VMEM((chips, blocks, modes, 128), BF16),
            pltpu.VMEM((chips, blocks, modes, 128), BF16),
            pltpu.VMEM((chips, blocks, modes, 128), BF16),
            pltpu.VMEM((chips, blocks, modes, 128), BF16),
            pltpu.VMEM((cols, share, modes, 128), BF16),
            pltpu.VMEM((cols, share, modes, 128), BF16),
            pltpu.VMEM((2, chips, blocks, modes, 128), BF16),
        ] + [pltpu.SemaphoreType.DMA((n,)) for n in counts],
        compiler_params=pltpu.CompilerParams(
            collective_id=0, has_side_effects=True, vmem_limit_bytes=60 * 1024 * 1024
        ),
    )(lie, snap, start_block.T)
    step = 8
    return pl.pallas_call(
        functools.partial(widen, scale),
        grid=(2 * chips * blocks // step,),
        out_shape=jax.ShapeDtypeStruct((modes, modes * modes), F32),
        in_specs=[pl.BlockSpec((step, modes, 128), lambda n: (n, 0, 0))],
        out_specs=pl.BlockSpec((modes, step * 128), lambda n: (0, n)),
    )(tensor)


def solution(mesh):
    chips, cols = mesh.shape["row"] // 2, mesh.shape["col"]
    return jax.shard_map(
        functools.partial(body, chips, cols),
        mesh=mesh,
        in_specs=(P("row", "col", None, None, None), P("row", "col", None, None, None), P()),
        out_specs=P(),
        check_vma=False,
    )
```

```python
import functools
import math

import jax
import jax.numpy as jnp
from jax import lax
from jax.experimental import pallas as pl
from jax.experimental.pallas import tpu as pltpu
from jax.sharding import PartitionSpec as P

ITERS = 4
MESH = pl.DeviceIdType.MESH
F32 = jnp.float32
BF16 = jnp.bfloat16
NT = (((1,), (1,)), ((), ()))


def neighbour_columns(nx, ny, nz):
    plane = ny * nz
    cells = nx * plane
    slab = 16
    cell = lax.broadcasted_iota(jnp.int32, (1, cells), 1)
    x, y, z = cell // plane, lax.rem(cell // nz, ny), lax.rem(cell, nz)
    x_before, x_after = cells, cells + plane
    y_before = cells + 2 * plane
    y_after = y_before + nx * slab
    ahead = [
        jnp.where(x < nx - 1, cell + plane, x_after + y * nz + z),
        jnp.where(y < ny - 1, cell + nz, y_after + x * slab + z),
        jnp.where(z < nz - 1, cell + 1, cell - (nz - 1)),
    ]
    behind = [
        jnp.where(x > 0, cell - plane, x_before + y * nz + z),
        jnp.where(y > 0, cell - nz, y_before + x * slab + slab - nz + z),
        jnp.where(z > 0, cell - 1, cell + nz - 1),
    ]
    return ahead, behind


def halves(value):
    high = value.astype(BF16)
    return high, (value - high.astype(F32)).astype(BF16)


def wide_left(value):
    high, low = halves(value)
    return jnp.concatenate([high, high, low], axis=1)


def kernel(
    chips, cols, span,
    lie_hbm, snap_hbm, start_hbm, out_ref,
    lie_ref, snap_ref, start_ref, loads, stores, sk_ref, sk_cols, hx, hy, sc1, rc1, acc1, rc2, rc3, cfull,
    diff, phi, phi_all, grad, adv,
    sg1, rg1, sg2, rg2, sg3, rg3, gfull,
    hs, hr, a1s, a1r, a2s, a2r, a3s, a3r, a4s, a4r, a5s, a5r,
    g1s, g1r, g2s, g2r, g3s, g3r, g4s, g4r, g5s, g5r, g6s, g6r,
):
    rows = 2 * chips
    row, col = lax.axis_index("row"), lax.axis_index("col")
    chip, core = row // 2, lax.rem(row, 2)
    sibling = (row + 1 - 2 * core, col)
    row_up, row_down = lax.rem(row + 1, rows), lax.rem(row + rows - 1, rows)
    col_up, col_down = lax.rem(col + 1, cols), lax.rem(col + cols - 1, cols)
    row_other = lax.rem(row + rows + 2 * core - 1, rows)

    def chip_at(offset):
        return lax.rem(chip + offset, chips)

    def col_at(offset):
        return lax.rem(col + offset, cols)

    def on_chip(q):
        return (2 * q + core, col)

    def push(src, dst, send, recv, device):
        return pltpu.make_async_remote_copy(
            src_ref=src, dst_ref=dst, send_sem=send, recv_sem=recv,
            device_id=device, device_id_type=MESH,
        )

    fetches = [
        pltpu.make_async_copy(src, dst, loads.at[n])
        for n, (src, dst) in enumerate(
            [(snap_hbm, snap_ref), (lie_hbm, lie_ref), (start_hbm, start_ref)]
        )
    ]
    for copy in fetches:
        copy.start()
    barrier = pltpu.get_barrier_semaphore()
    partners = [sibling, (row_other, col)]
    partners += [on_chip(chip_at(o)) for o in range(1, chips)]
    partners += [(row, col_at(o)) for o in range(1, cols)]
    for device in partners:
        pl.semaphore_signal(barrier, inc=1, device_id=device, device_id_type=MESH)

    comps, rank = sk_ref.shape[0], sk_ref.shape[-1]
    for copy in fetches:
        copy.wait()
    snaps = snap_ref[...].reshape(-1, snap_ref.shape[-1])
    sk_cols[...] = lie_ref[...].reshape(-1, rank).T.reshape(sk_cols.shape)
    for c in range(comps):
        sk_ref[c] = lie_ref[:, c].reshape(sk_ref.shape[1:])

    waves = range(sc1.shape[0])

    def projection(which):
        half = jnp.dot(sk_cols[which], snaps, preferred_element_type=F32)
        size = sc1.shape[-1]
        return [half[:, w * size:(w + 1) * size].reshape(sc1.shape[1:]) for w in waves]

    for w, value in enumerate(projection(1 - core)):
        sc1[w] = value
    pl.semaphore_wait(barrier, len(partners))
    a1 = [push(sc1.at[w], rc1.at[w], a1s.at[w], a1r.at[w], sibling) for w in waves]
    for copy in a1:
        copy.start()
    nx, plane = sk_ref.shape[1:3]
    halos = [
        push(sk_ref.at[:, nx - 1], hx.at[0], hs.at[0], hr.at[0], (row_up, col)),
        push(sk_ref.at[:, 0], hx.at[1], hs.at[1], hr.at[1], (row_down, col)),
        push(sk_ref.at[:, :, pl.ds(plane - 16, 16)], hy.at[0], hs.at[2], hr.at[2], (row, col_up)),
        push(sk_ref.at[:, :, pl.ds(0, 16)], hy.at[1], hs.at[3], hr.at[3], (row, col_down)),
    ]
    for copy in halos:
        copy.start()
    mine = projection(core)
    a2 = []
    for w in waves:
        a1[w].wait_recv()
        acc1[w] = mine[w] + rc1[w]
        for o in range(1, chips):
            q = chip_at(o)
            copy = push(
                acc1.at[w, q], rc2.at[w, chip],
                a2s.at[w * chips + o], a2r.at[w * chips + chip], on_chip(q),
            )
            copy.start()
            a2.append(copy)

    extent = diff.shape[0]
    cells = nx * plane
    place = lax.broadcasted_iota(jnp.int32, (extent, cells), 0)
    for d, (fore, aft) in enumerate(zip(*neighbour_columns(nx, plane // span, span))):
        diff[:, d * cells:(d + 1) * cells] = (
            jnp.where(place == fore, 0.5, 0.0) - jnp.where(place == aft, 0.5, 0.0)
        ).astype(BF16)

    a3 = []
    for w in waves:
        total = acc1[w, chip]
        for o in range(1, chips):
            q = chip_at(o)
            block = rc2.at[w, q]
            push(block, block, a2s.at[0], a2r.at[w * chips + q], sibling).wait_recv()
            total = total + rc2[w, q]
        rc3[w, col] = total
        own = rc3.at[w, col]
        for o in range(1, cols):
            copy = push(
                own, own, a3s.at[w * cols + o], a3r.at[w * cols + col], (row, col_at(o))
            )
            copy.start()
            a3.append(copy)
    a4, a5 = [], []
    for w in waves:
        for o in range(1, cols):
            z = col_at(o)
            block = rc3.at[w, z]
            push(block, block, a3s.at[0], a3r.at[w * cols + z], sibling).wait_recv()
        total = rc3[w, 0]
        for z in range(1, cols):
            total = total + rc3[w, z]
        cfull[w, core, chip] = total
        own = cfull.at[w, core, chip]
        for o in range(1, chips):
            copy = push(
                own, own, a4s.at[w * chips + o], a4r.at[w * chips + chip], on_chip(chip_at(o))
            )
            copy.start()
            a4.append(copy)
        copy = push(own, own, a5s.at[w * chips], a5r.at[w * chips + chip], sibling)
        copy.start()
        a5.append(copy)
    for w in waves:
        for o in range(1, chips):
            q = chip_at(o)
            block = cfull.at[w, core, q]
            push(block, block, a4s.at[0], a4r.at[w * chips + q], sibling).wait_recv()
            copy = push(block, block, a5s.at[w * chips + o], a5r.at[w * chips + q], sibling)
            copy.start()
            a5.append(copy)
    for w in waves:
        for q in range(chips):
            block = cfull.at[w, 1 - core, q]
            push(block, block, a5s.at[0], a5r.at[w * chips + q], sibling).wait_recv()

    coeffs = jnp.concatenate([cfull[w].reshape(rank, -1) for w in waves], axis=1)
    start = start_ref[...]
    modes, rank = start.shape
    coeffs_h, coeffs_l = halves(coeffs)
    projected = jnp.dot(
        wide_left(start),
        jnp.concatenate([coeffs_h, coeffs_l, coeffs_h], axis=0),
        preferred_element_type=F32,
    )
    y_matrix = lax.dot_general(
        wide_left(projected),
        jnp.concatenate([coeffs_h, coeffs_l, coeffs_h], axis=1),
        NT, preferred_element_type=F32,
    )
    polar = y_matrix / jnp.sqrt(jnp.sum(y_matrix * y_matrix) + 1e-06)
    polar = jnp.concatenate([polar, jnp.zeros((-modes % 128, rank), F32)], axis=0)
    for _ in range(ITERS):
        high, low = halves(polar)
        gram = lax.dot_general(
            jnp.concatenate([high, high, low], axis=1),
            jnp.concatenate([high, low, high], axis=1),
            NT, preferred_element_type=F32,
        )
        polar = 1.5 * polar - 0.5 * jnp.dot(
            wide_left(gram),
            jnp.concatenate([high, low, high], axis=0),
            preferred_element_type=F32,
        )
    polar = polar[:modes]
    basis = polar.astype(BF16)

    for copy in halos:
        copy.wait_recv()
    for c in range(3):
        inner = sk_ref[c].reshape(cells, rank)
        outer = jnp.concatenate(
            [hx[0, c], hx[1, c], hy[0, c].reshape(-1, rank), hy[1, c].reshape(-1, rank)], axis=0
        )
        field = lax.dot_general(basis, inner, NT, preferred_element_type=F32).astype(BF16)
        rim = lax.dot_general(basis, outer, NT, preferred_element_type=F32).astype(BF16)
        phi[c] = field.astype(F32).reshape(phi.shape[1:])
        phi_all[c * cells:(c + 1) * cells] = lax.dot_general(
            inner, basis, NT, preferred_element_type=F32
        ).astype(BF16)
        slopes = jnp.dot(
            jnp.concatenate([field, rim], axis=1), diff[...], preferred_element_type=F32
        ).astype(BF16)
        for d in range(3):
            grad[d, c] = slopes[:, d * cells:(d + 1) * cells]

    blocks = gfull.shape[2]
    count = 128 * blocks // modes

    def part(which, q):
        group_at = which * chips + q
        for ct in range(cells // 128):
            lanes = slice(ct * 128, ct * 128 + 128)
            for group in range(0, count, 4):
                some = range(group, min(group + 4, count))
                p = [
                    [
                        jnp.broadcast_to(phi[d, group_at, i:i + 1, lanes], (16, 128)).astype(BF16)
                        for d in range(3)
                    ]
                    for i in some
                ]
                for c in range(3):
                    for jt in range(0, modes, 16):
                        g = [grad[d, c, jt:jt + 16, lanes] for d in range(3)]
                        for i, pi in zip(some, p):
                            adv[
                                i * modes + jt:i * modes + jt + 16,
                                c * cells + ct * 128:c * cells + ct * 128 + 128,
                            ] = pi[0] * g[0] + pi[1] * g[1] + pi[2] * g[2]
        value = jnp.dot(adv[...], phi_all[...], preferred_element_type=F32)
        return [value[n * 128:n * 128 + 128].T for n in range(blocks)]

    def theirs(step, carry):
        q = chip_at(step + 1)
        for n, value in enumerate(part(1 - core, q)):
            sg1[q, n] = value.astype(BF16)
        push(sg1.at[q], rg1.at[q], g1s.at[q], g1r.at[q], sibling).start()
        return carry

    lax.fori_loop(0, chips, theirs, 0)

    def ours(q):
        values = part(core, q)
        push(rg1.at[q], rg1.at[q], g1s.at[q], g1r.at[q], sibling).wait_recv()
        return [value + rg1[q, n].astype(F32) for n, value in enumerate(values)]

    def for_others(step, carry):
        q = chip_at(step + 1)
        for n, value in enumerate(ours(q)):
            sg2[q, n] = value.astype(BF16)
        push(sg2.at[q], rg2.at[chip], g2s.at[q], g2r.at[chip], on_chip(q)).start()
        return carry

    lax.fori_loop(0, chips - 1, for_others, 0)
    sums = ours(chip)
    for o in range(1, chips):
        q = chip_at(o)
        push(rg2.at[q], rg2.at[q], g2s.at[q], g2r.at[q], sibling).wait_recv()
        sums = [value + rg2[q, n].astype(F32) for n, value in enumerate(sums)]

    share = blocks // cols
    later = []
    if share:
        for n, value in enumerate(sums):
            sg3[n // share, n % share] = value.astype(BF16)
        for o in range(1, cols):
            z = col_at(o)
            copy = push(sg3.at[z], rg3.at[col], g3s.at[z], g3r.at[col], (row, z))
            copy.start()
            later.append(copy)
        final = sg3[col].astype(F32)
        for o in range(1, cols):
            z = col_at(o)
            push(rg3.at[z], rg3.at[z], g3s.at[z], g3r.at[z], sibling).wait_recv()
            final = final + rg3[z].astype(F32)
        gfull[core, chip, pl.ds(col * share, share)] = final.astype(BF16)
        own = gfull.at[core, chip, pl.ds(col * share, share)]
        for o in range(1, cols):
            z = col_at(o)
            copy = push(own, own, g4s.at[z], g4r.at[col], (row, z))
            copy.start()
            later.append(copy)
    else:
        for n, value in enumerate(sums):
            rg3[col, n] = value.astype(BF16)
        for o in range(1, cols):
            z = col_at(o)
            copy = push(rg3.at[col], rg3.at[col], g3s.at[z], g3r.at[col], (row, z))
            copy.start()
            later.append(copy)
        for o in range(1, cols):
            z = col_at(o)
            push(rg3.at[z], rg3.at[z], g3s.at[z], g3r.at[z], sibling).wait_recv()
        final = rg3[0].astype(F32)
        for z in range(1, cols):
            final = final + rg3[z].astype(F32)
        gfull[core, chip] = final.astype(BF16)

    pieces = cols if share else 1
    width = blocks // pieces

    def piece(which, q, z):
        return gfull.at[which, q, pl.ds(z * width, width)]

    outs = []

    def write(which, q, z):
        for n in range(width):
            block = z * width + n
            slot = (which * chips + q) * blocks + block
            lanes = pl.ds(pl.multiple_of(slot * 128, 128), 128)
            copy = pltpu.make_async_copy(
                gfull.at[which, q, block], out_ref.at[:, lanes], stores.at[slot]
            )
            copy.start()
            outs.append(copy)

    def forward(q, z):
        part_of = piece(core, q, z)
        copy = push(part_of, part_of, g6s.at[q * pieces + z], g6r.at[q * pieces + z], sibling)
        copy.start()
        later.append(copy)
        write(core, q, z)

    order = [col_at(o) for o in range(pieces)] if share else [0]
    for o, z in enumerate(order):
        own = piece(core, chip, z)
        if o:
            push(own, own, g4s.at[z], g4r.at[z], sibling).wait_recv()
        for offset in range(1, chips):
            q = chip_at(offset)
            copy = push(
                own, own, g5s.at[q * pieces + z], g5r.at[chip * pieces + z], on_chip(q)
            )
            copy.start()
            later.append(copy)
        forward(chip, z)
    for z in order:
        for offset in range(1, chips):
            q = chip_at(offset)
            block = piece(core, q, z)
            slot = q * pieces + z
            push(block, block, g5s.at[slot], g5r.at[slot], sibling).wait_recv()
            forward(q, z)
    for z in order:
        for offset in range(chips):
            q = chip_at(offset)
            block = piece(1 - core, q, z)
            slot = q * pieces + z
            push(block, block, g6s.at[slot], g6r.at[slot], sibling).wait_recv()
            write(1 - core, q, z)

    for copy in outs:
        copy.wait()
    for copy in [*a1, *halos, *a2, *a3, *a4, *a5, *later]:
        copy.wait_send()
    for q in range(chips):
        push(sg1.at[q], rg1.at[q], g1s.at[q], g1r.at[q], sibling).wait_send()
    for o in range(1, chips):
        q = chip_at(o)
        push(sg2.at[q], rg2.at[q], g2s.at[q], g2r.at[q], sibling).wait_send()


def body(chips, cols, sketch, snapshots, start_block):
    nx, ny, nz, comps, rank = sketch.shape
    snaps = snapshots.shape[-1]
    modes = start_block.shape[1]
    cells = nx * ny * nz
    depth = rank // (2 * chips)
    lie = sketch.transpose(0, 1, 3, 2, 4).reshape(nx * ny, comps, nz, rank)
    snap = snapshots.transpose(0, 1, 3, 2, 4).reshape(nx * ny * comps, nz, snaps)
    extent = cells + 2 * ny * nz + 2 * nx * 16
    blocks = modes * modes // (2 * chips * 128)
    share = max(blocks // cols, 1)
    scale = 1.0 / math.sqrt(cells * 2 * chips * cols)
    waves = 2
    counts = [4, 4, waves, waves] + [waves * chips] * 2 + [waves * cols] * 2
    counts += [waves * chips] * 4
    pieces = cols if blocks // cols else 1
    counts += [chips] * 4 + [cols] * 4 + [chips * pieces] * 4
    tensor = pl.pallas_call(
        functools.partial(kernel, chips, cols, nz),
        out_shape=jax.ShapeDtypeStruct((modes, modes * modes), BF16),
        in_specs=[pl.BlockSpec(memory_space=pltpu.HBM)] * 3,
        out_specs=pl.BlockSpec(memory_space=pltpu.HBM),
        scratch_shapes=[
            pltpu.VMEM(lie.shape, BF16),
            pltpu.VMEM(snap.shape, BF16),
            pltpu.VMEM((modes, rank), F32),
            pltpu.SemaphoreType.DMA((3,)),
            pltpu.SemaphoreType.DMA((2 * chips * blocks,)),
            pltpu.VMEM((comps, nx, ny * nz, rank), BF16),
            pltpu.VMEM((2, rank // 2, comps * cells), BF16),
            pltpu.VMEM((2, comps, ny * nz, rank), BF16),
            pltpu.VMEM((2, comps, nx, 16, rank), BF16),
            pltpu.VMEM((waves, chips, depth, snaps // waves), F32),
            pltpu.VMEM((waves, chips, depth, snaps // waves), F32),
            pltpu.VMEM((waves, chips, depth, snaps // waves), F32),
            pltpu.VMEM((waves, chips, depth, snaps // waves), F32),
            pltpu.VMEM((waves, cols, depth, snaps // waves), F32),
            pltpu.VMEM((waves, 2, chips, depth, snaps // waves), F32),
            pltpu.VMEM((extent, 3 * cells), BF16),
            pltpu.VMEM((comps, 2 * chips, modes // (2 * chips), cells), F32),
            pltpu.VMEM((comps * cells, modes), BF16),
            pltpu.VMEM((3, comps, modes, cells), BF16),
            pltpu.VMEM((blocks * 128, comps * cells), BF16),
            pltpu.VMEM((chips, blocks, modes, 128), BF16),
            pltpu.VMEM((chips, blocks, modes, 128), BF16),
            pltpu.VMEM((chips, blocks, modes, 128), BF16),
            pltpu.VMEM((chips, blocks, modes, 128), BF16),
            pltpu.VMEM((cols, share, modes, 128), BF16),
            pltpu.VMEM((cols, share, modes, 128), BF16),
            pltpu.VMEM((2, chips, blocks, modes, 128), BF16),
        ] + [pltpu.SemaphoreType.DMA((n,)) for n in counts],
        compiler_params=pltpu.CompilerParams(
            collective_id=0, has_side_effects=True, vmem_limit_bytes=60 * 1024 * 1024
        ),
    )(lie, snap, start_block.T)
    return tensor.astype(F32) * scale


def solution(mesh):
    chips, cols = mesh.shape["row"] // 2, mesh.shape["col"]
    return jax.shard_map(
        functools.partial(body, chips, cols),
        mesh=mesh,
        in_specs=(P("row", "col", None, None, None), P("row", "col", None, None, None), P()),
        out_specs=P(),
        check_vma=False,
    )
```

```python
import functools
import math

import jax
import jax.numpy as jnp
from jax import lax
from jax.experimental import pallas as pl
from jax.experimental.pallas import tpu as pltpu
from jax.sharding import PartitionSpec as P

ITERS = 4
MESH = pl.DeviceIdType.MESH
F32 = jnp.float32
BF16 = jnp.bfloat16
NT = (((1,), (1,)), ((), ()))


def neighbour_columns(nx, ny, nz):
    plane = ny * nz
    cells = nx * plane
    slab = 16
    cell = lax.broadcasted_iota(jnp.int32, (1, cells), 1)
    x, y, z = cell // plane, lax.rem(cell // nz, ny), lax.rem(cell, nz)
    x_before, x_after = cells, cells + plane
    y_before = cells + 2 * plane
    y_after = y_before + nx * slab
    ahead = [
        jnp.where(x < nx - 1, cell + plane, x_after + y * nz + z),
        jnp.where(y < ny - 1, cell + nz, y_after + x * slab + z),
        jnp.where(z < nz - 1, cell + 1, cell - (nz - 1)),
    ]
    behind = [
        jnp.where(x > 0, cell - plane, x_before + y * nz + z),
        jnp.where(y > 0, cell - nz, y_before + x * slab + slab - nz + z),
        jnp.where(z > 0, cell - 1, cell + nz - 1),
    ]
    return ahead, behind


def halves(value):
    high = value.astype(BF16)
    return high, (value - high.astype(F32)).astype(BF16)


def wide_left(value):
    high, low = halves(value)
    return jnp.concatenate([high, high, low], axis=1)


def kernel(
    chips, cols, span,
    lie_hbm, snap_hbm, start_hbm, out_ref,
    lie_ref, snap_ref, start_ref, loads, stores, sk_ref, sk_cols, hx, hy, sc1, rc1, acc1, rc2, rc3, cfull,
    diff, phi, phi_all, grad, adv,
    sg1, rg1, sg2, rg2, sg3, rg3, gfull,
    hs, hr, a1s, a1r, a2s, a2r, a3s, a3r, a4s, a4r,
    g1s, g1r, g2s, g2r, g3s, g3r, g4s, g4r, g5s, g5r, g6s, g6r,
):
    rows = 2 * chips
    row, col = lax.axis_index("row"), lax.axis_index("col")
    chip, core = row // 2, lax.rem(row, 2)
    sibling = (row + 1 - 2 * core, col)
    row_up, row_down = lax.rem(row + 1, rows), lax.rem(row + rows - 1, rows)
    col_up, col_down = lax.rem(col + 1, cols), lax.rem(col + cols - 1, cols)

    def chip_at(offset):
        return lax.rem(chip + offset, chips)

    def col_at(offset):
        return lax.rem(col + offset, cols)

    def on_chip(q):
        return (2 * q + core, col)

    def push(src, dst, send, recv, device):
        return pltpu.make_async_remote_copy(
            src_ref=src, dst_ref=dst, send_sem=send, recv_sem=recv,
            device_id=device, device_id_type=MESH,
        )

    fetches = [
        pltpu.make_async_copy(src, dst, loads.at[n])
        for n, (src, dst) in enumerate(
            [(snap_hbm, snap_ref), (lie_hbm, lie_ref), (start_hbm, start_ref)]
        )
    ]
    for copy in fetches:
        copy.start()
    barrier = pltpu.get_barrier_semaphore()
    partners = [(lax.rem(row + o, rows), col) for o in range(1, rows)]
    partners += [(row, col_at(o)) for o in range(1, cols)]
    for device in partners:
        pl.semaphore_signal(barrier, inc=1, device_id=device, device_id_type=MESH)

    comps, rank = sk_ref.shape[0], sk_ref.shape[-1]
    for copy in fetches:
        copy.wait()
    snaps = snap_ref[...].reshape(-1, snap_ref.shape[-1])
    sk_cols[...] = lie_ref[...].reshape(-1, rank).T.reshape(sk_cols.shape)
    for c in range(comps):
        sk_ref[c] = lie_ref[:, c].reshape(sk_ref.shape[1:])

    waves = range(sc1.shape[0])

    def projection(which):
        half = jnp.dot(sk_cols[which], snaps, preferred_element_type=F32)
        size = sc1.shape[-1]
        return [half[:, w * size:(w + 1) * size].reshape(sc1.shape[1:]) for w in waves]

    for w, value in enumerate(projection(1 - core)):
        sc1[w] = value
    pl.semaphore_wait(barrier, len(partners))
    a1 = [push(sc1.at[w], rc1.at[w], a1s.at[w], a1r.at[w], sibling) for w in waves]
    for copy in a1:
        copy.start()
    nx, plane = sk_ref.shape[1:3]
    halos = [
        push(sk_ref.at[:, nx - 1], hx.at[0], hs.at[0], hr.at[0], (row_up, col)),
        push(sk_ref.at[:, 0], hx.at[1], hs.at[1], hr.at[1], (row_down, col)),
        push(sk_ref.at[:, :, pl.ds(plane - 16, 16)], hy.at[0], hs.at[2], hr.at[2], (row, col_up)),
        push(sk_ref.at[:, :, pl.ds(0, 16)], hy.at[1], hs.at[3], hr.at[3], (row, col_down)),
    ]
    for copy in halos:
        copy.start()
    mine = projection(core)
    a2 = []
    for w in waves:
        a1[w].wait_recv()
        acc1[w] = mine[w] + rc1[w]
        for o in range(1, chips):
            q = chip_at(o)
            copy = push(
                acc1.at[w, q], rc2.at[w, chip],
                a2s.at[w * chips + o], a2r.at[w * chips + chip], on_chip(q),
            )
            copy.start()
            a2.append(copy)

    extent = diff.shape[0]
    cells = nx * plane
    place = lax.broadcasted_iota(jnp.int32, (extent, cells), 0)
    for d, (fore, aft) in enumerate(zip(*neighbour_columns(nx, plane // span, span))):
        diff[:, d * cells:(d + 1) * cells] = (
            jnp.where(place == fore, 0.5, 0.0) - jnp.where(place == aft, 0.5, 0.0)
        ).astype(BF16)

    a3 = []
    for w in waves:
        total = acc1[w, chip]
        for o in range(1, chips):
            q = chip_at(o)
            block = rc2.at[w, q]
            push(block, block, a2s.at[0], a2r.at[w * chips + q], sibling).wait_recv()
            total = total + rc2[w, q]
        rc3[w, col] = total
        own = rc3.at[w, col]
        for o in range(1, cols):
            copy = push(
                own, own, a3s.at[w * cols + o], a3r.at[w * cols + col], (row, col_at(o))
            )
            copy.start()
            a3.append(copy)
    a4 = []
    for w in waves:
        for o in range(1, cols):
            z = col_at(o)
            block = rc3.at[w, z]
            push(block, block, a3s.at[0], a3r.at[w * cols + z], sibling).wait_recv()
        total = rc3[w, 0]
        for z in range(1, cols):
            total = total + rc3[w, z]
        cfull[w, core, chip] = total
        own = cfull.at[w, core, chip]
        for o in range(1, rows):
            copy = push(
                own, own, a4s.at[w * rows + o], a4r.at[w * rows + row],
                (lax.rem(row + o, rows), col),
            )
            copy.start()
            a4.append(copy)
    for w in waves:
        for o in range(1, rows):
            r = lax.rem(row + o, rows)
            block = cfull.at[w, lax.rem(r, 2), r // 2]
            push(block, block, a4s.at[0], a4r.at[w * rows + r], sibling).wait_recv()

    coeffs = jnp.concatenate([cfull[w].reshape(rank, -1) for w in waves], axis=1)
    start = start_ref[...]
    modes, rank = start.shape
    coeffs_h, coeffs_l = halves(coeffs)
    projected = jnp.dot(
        wide_left(start),
        jnp.concatenate([coeffs_h, coeffs_l, coeffs_h], axis=0),
        preferred_element_type=F32,
    )
    y_matrix = lax.dot_general(
        wide_left(projected),
        jnp.concatenate([coeffs_h, coeffs_l, coeffs_h], axis=1),
        NT, preferred_element_type=F32,
    )
    polar = y_matrix / jnp.sqrt(jnp.sum(y_matrix * y_matrix) + 1e-06)
    polar = jnp.concatenate([polar, jnp.zeros((-modes % 128, rank), F32)], axis=0)
    for _ in range(ITERS):
        high, low = halves(polar)
        gram = lax.dot_general(
            jnp.concatenate([high, high, low], axis=1),
            jnp.concatenate([high, low, high], axis=1),
            NT, preferred_element_type=F32,
        )
        polar = 1.5 * polar - 0.5 * jnp.dot(
            wide_left(gram),
            jnp.concatenate([high, low, high], axis=0),
            preferred_element_type=F32,
        )
    polar = polar[:modes]
    basis = polar.astype(BF16)

    for copy in halos:
        copy.wait_recv()
    for c in range(3):
        inner = sk_ref[c].reshape(cells, rank)
        outer = jnp.concatenate(
            [hx[0, c], hx[1, c], hy[0, c].reshape(-1, rank), hy[1, c].reshape(-1, rank)], axis=0
        )
        field = lax.dot_general(basis, inner, NT, preferred_element_type=F32).astype(BF16)
        rim = lax.dot_general(basis, outer, NT, preferred_element_type=F32).astype(BF16)
        phi[c] = field.astype(F32).reshape(phi.shape[1:])
        phi_all[c * cells:(c + 1) * cells] = lax.dot_general(
            inner, basis, NT, preferred_element_type=F32
        ).astype(BF16)
        slopes = jnp.dot(
            jnp.concatenate([field, rim], axis=1), diff[...], preferred_element_type=F32
        ).astype(BF16)
        for d in range(3):
            grad[d, c] = slopes[:, d * cells:(d + 1) * cells]

    blocks = gfull.shape[2]
    count = 128 * blocks // modes

    def part(which, q):
        group_at = which * chips + q
        for ct in range(cells // 128):
            lanes = slice(ct * 128, ct * 128 + 128)
            for group in range(0, count, 4):
                some = range(group, min(group + 4, count))
                p = [
                    [
                        jnp.broadcast_to(phi[d, group_at, i:i + 1, lanes], (16, 128)).astype(BF16)
                        for d in range(3)
                    ]
                    for i in some
                ]
                for c in range(3):
                    for jt in range(0, modes, 16):
                        g = [grad[d, c, jt:jt + 16, lanes] for d in range(3)]
                        for i, pi in zip(some, p):
                            adv[
                                i * modes + jt:i * modes + jt + 16,
                                c * cells + ct * 128:c * cells + ct * 128 + 128,
                            ] = pi[0] * g[0] + pi[1] * g[1] + pi[2] * g[2]
        value = jnp.dot(adv[...], phi_all[...], preferred_element_type=F32)
        return [value[n * 128:n * 128 + 128].T for n in range(blocks)]

    def theirs(step, carry):
        q = chip_at(step + 1)
        for n, value in enumerate(part(1 - core, q)):
            sg1[q, n] = value.astype(BF16)
        push(sg1.at[q], rg1.at[q], g1s.at[q], g1r.at[q], sibling).start()
        return carry

    lax.fori_loop(0, chips, theirs, 0)

    def ours(q):
        values = part(core, q)
        push(rg1.at[q], rg1.at[q], g1s.at[q], g1r.at[q], sibling).wait_recv()
        return [value + rg1[q, n].astype(F32) for n, value in enumerate(values)]

    def for_others(step, carry):
        q = chip_at(step + 1)
        for n, value in enumerate(ours(q)):
            sg2[q, n] = value.astype(BF16)
        push(sg2.at[q], rg2.at[chip], g2s.at[q], g2r.at[chip], on_chip(q)).start()
        return carry

    lax.fori_loop(0, chips - 1, for_others, 0)
    sums = ours(chip)
    for o in range(1, chips):
        q = chip_at(o)
        push(rg2.at[q], rg2.at[q], g2s.at[q], g2r.at[q], sibling).wait_recv()
        sums = [value + rg2[q, n].astype(F32) for n, value in enumerate(sums)]

    share = blocks // cols
    later = []
    if share:
        for n, value in enumerate(sums):
            sg3[n // share, n % share] = value.astype(BF16)
        for o in range(1, cols):
            z = col_at(o)
            copy = push(sg3.at[z], rg3.at[col], g3s.at[z], g3r.at[col], (row, z))
            copy.start()
            later.append(copy)
        final = sg3[col].astype(F32)
        for o in range(1, cols):
            z = col_at(o)
            push(rg3.at[z], rg3.at[z], g3s.at[z], g3r.at[z], sibling).wait_recv()
            final = final + rg3[z].astype(F32)
        gfull[core, chip, pl.ds(col * share, share)] = final.astype(BF16)
        own = gfull.at[core, chip, pl.ds(col * share, share)]
        for o in range(1, cols):
            z = col_at(o)
            copy = push(own, own, g4s.at[z], g4r.at[col], (row, z))
            copy.start()
            later.append(copy)
    else:
        for n, value in enumerate(sums):
            rg3[col, n] = value.astype(BF16)
        for o in range(1, cols):
            z = col_at(o)
            copy = push(rg3.at[col], rg3.at[col], g3s.at[z], g3r.at[col], (row, z))
            copy.start()
            later.append(copy)
        for o in range(1, cols):
            z = col_at(o)
            push(rg3.at[z], rg3.at[z], g3s.at[z], g3r.at[z], sibling).wait_recv()
        final = rg3[0].astype(F32)
        for z in range(1, cols):
            final = final + rg3[z].astype(F32)
        gfull[core, chip] = final.astype(BF16)

    pieces = cols if share else 1
    width = blocks // pieces

    def piece(which, q, z):
        return gfull.at[which, q, pl.ds(z * width, width)]

    outs = []

    def write(which, q, z):
        for n in range(width):
            block = z * width + n
            slot = (which * chips + q) * blocks + block
            lanes = pl.ds(pl.multiple_of(slot * 128, 128), 128)
            copy = pltpu.make_async_copy(
                gfull.at[which, q, block], out_ref.at[:, lanes], stores.at[slot]
            )
            copy.start()
            outs.append(copy)

    def forward(q, z):
        part_of = piece(core, q, z)
        copy = push(part_of, part_of, g6s.at[q * pieces + z], g6r.at[q * pieces + z], sibling)
        copy.start()
        later.append(copy)
        write(core, q, z)

    order = [col_at(o) for o in range(pieces)] if share else [0]
    for o, z in enumerate(order):
        own = piece(core, chip, z)
        if o:
            push(own, own, g4s.at[z], g4r.at[z], sibling).wait_recv()
        for offset in range(1, chips):
            q = chip_at(offset)
            copy = push(
                own, own, g5s.at[q * pieces + z], g5r.at[chip * pieces + z], on_chip(q)
            )
            copy.start()
            later.append(copy)
        forward(chip, z)
    for z in order:
        for offset in range(1, chips):
            q = chip_at(offset)
            block = piece(core, q, z)
            slot = q * pieces + z
            push(block, block, g5s.at[slot], g5r.at[slot], sibling).wait_recv()
            forward(q, z)
    for z in order:
        for offset in range(chips):
            q = chip_at(offset)
            block = piece(1 - core, q, z)
            slot = q * pieces + z
            push(block, block, g6s.at[slot], g6r.at[slot], sibling).wait_recv()
            write(1 - core, q, z)

    for copy in outs:
        copy.wait()
    for copy in [*a1, *halos, *a2, *a3, *a4, *later]:
        copy.wait_send()
    for q in range(chips):
        push(sg1.at[q], rg1.at[q], g1s.at[q], g1r.at[q], sibling).wait_send()
    for o in range(1, chips):
        q = chip_at(o)
        push(sg2.at[q], rg2.at[q], g2s.at[q], g2r.at[q], sibling).wait_send()


def body(chips, cols, sketch, snapshots, start_block):
    nx, ny, nz, comps, rank = sketch.shape
    snaps = snapshots.shape[-1]
    modes = start_block.shape[1]
    cells = nx * ny * nz
    depth = rank // (2 * chips)
    lie = sketch.transpose(0, 1, 3, 2, 4).reshape(nx * ny, comps, nz, rank)
    snap = snapshots.transpose(0, 1, 3, 2, 4).reshape(nx * ny * comps, nz, snaps)
    extent = cells + 2 * ny * nz + 2 * nx * 16
    blocks = modes * modes // (2 * chips * 128)
    share = max(blocks // cols, 1)
    scale = 1.0 / math.sqrt(cells * 2 * chips * cols)
    waves = 2
    counts = [4, 4, waves, waves] + [waves * chips] * 2 + [waves * cols] * 2
    counts += [waves * 2 * chips] * 2
    pieces = cols if blocks // cols else 1
    counts += [chips] * 4 + [cols] * 4 + [chips * pieces] * 4
    tensor = pl.pallas_call(
        functools.partial(kernel, chips, cols, nz),
        out_shape=jax.ShapeDtypeStruct((modes, modes * modes), BF16),
        in_specs=[pl.BlockSpec(memory_space=pltpu.HBM)] * 3,
        out_specs=pl.BlockSpec(memory_space=pltpu.HBM),
        scratch_shapes=[
            pltpu.VMEM(lie.shape, BF16),
            pltpu.VMEM(snap.shape, BF16),
            pltpu.VMEM((modes, rank), F32),
            pltpu.SemaphoreType.DMA((3,)),
            pltpu.SemaphoreType.DMA((2 * chips * blocks,)),
            pltpu.VMEM((comps, nx, ny * nz, rank), BF16),
            pltpu.VMEM((2, rank // 2, comps * cells), BF16),
            pltpu.VMEM((2, comps, ny * nz, rank), BF16),
            pltpu.VMEM((2, comps, nx, 16, rank), BF16),
            pltpu.VMEM((waves, chips, depth, snaps // waves), F32),
            pltpu.VMEM((waves, chips, depth, snaps // waves), F32),
            pltpu.VMEM((waves, chips, depth, snaps // waves), F32),
            pltpu.VMEM((waves, chips, depth, snaps // waves), F32),
            pltpu.VMEM((waves, cols, depth, snaps // waves), F32),
            pltpu.VMEM((waves, 2, chips, depth, snaps // waves), F32),
            pltpu.VMEM((extent, 3 * cells), BF16),
            pltpu.VMEM((comps, 2 * chips, modes // (2 * chips), cells), F32),
            pltpu.VMEM((comps * cells, modes), BF16),
            pltpu.VMEM((3, comps, modes, cells), BF16),
            pltpu.VMEM((blocks * 128, comps * cells), BF16),
            pltpu.VMEM((chips, blocks, modes, 128), BF16),
            pltpu.VMEM((chips, blocks, modes, 128), BF16),
            pltpu.VMEM((chips, blocks, modes, 128), BF16),
            pltpu.VMEM((chips, blocks, modes, 128), BF16),
            pltpu.VMEM((cols, share, modes, 128), BF16),
            pltpu.VMEM((cols, share, modes, 128), BF16),
            pltpu.VMEM((2, chips, blocks, modes, 128), BF16),
        ] + [pltpu.SemaphoreType.DMA((n,)) for n in counts],
        compiler_params=pltpu.CompilerParams(
            collective_id=0, has_side_effects=True, vmem_limit_bytes=60 * 1024 * 1024
        ),
    )(lie, snap, start_block.T)
    return tensor.astype(F32) * scale


def solution(mesh):
    chips, cols = mesh.shape["row"] // 2, mesh.shape["col"]
    return jax.shard_map(
        functools.partial(body, chips, cols),
        mesh=mesh,
        in_specs=(P("row", "col", None, None, None), P("row", "col", None, None, None), P()),
        out_specs=P(),
        check_vma=False,
    )
```

```python
import functools
import math

import jax
import jax.numpy as jnp
from jax import lax
from jax.experimental import pallas as pl
from jax.experimental.pallas import tpu as pltpu
from jax.sharding import PartitionSpec as P

ITERS = 4
MESH = pl.DeviceIdType.MESH
F32 = jnp.float32
BF16 = jnp.bfloat16
NT = (((1,), (1,)), ((), ()))


def neighbour_columns(nx, ny, nz):
    plane = ny * nz
    cells = nx * plane
    slab = 16
    cell = lax.broadcasted_iota(jnp.int32, (1, cells), 1)
    x, y, z = cell // plane, lax.rem(cell // nz, ny), lax.rem(cell, nz)
    x_before, x_after = cells, cells + plane
    y_before = cells + 2 * plane
    y_after = y_before + nx * slab
    ahead = [
        jnp.where(x < nx - 1, cell + plane, x_after + y * nz + z),
        jnp.where(y < ny - 1, cell + nz, y_after + x * slab + z),
        jnp.where(z < nz - 1, cell + 1, cell - (nz - 1)),
    ]
    behind = [
        jnp.where(x > 0, cell - plane, x_before + y * nz + z),
        jnp.where(y > 0, cell - nz, y_before + x * slab + slab - nz + z),
        jnp.where(z > 0, cell - 1, cell + nz - 1),
    ]
    return ahead, behind


def halves(value):
    high = value.astype(BF16)
    return high, (value - high.astype(F32)).astype(BF16)


def wide_left(value):
    high, low = halves(value)
    return jnp.concatenate([high, high, low], axis=1)


def kernel(
    chips, cols, span,
    lie_hbm, snap_hbm, start_hbm, out_ref,
    lie_ref, snap_ref, start_ref, loads, stores, sk_ref, sk_cols, hx, hy, sc1, rc1, acc1, rc2, rc3, cfull,
    diff, phi, phi_all, grad, adv,
    sg1, rg1, sg2, rg2, sg3, rg3, gfull,
    hs, hr, a1s, a1r, a2s, a2r, a3s, a3r, a4s, a4r, a5s, a5r,
    g1s, g1r, g2s, g2r, g3s, g3r, g4s, g4r, g5s, g5r, g6s, g6r,
):
    rows = 2 * chips
    row, col = lax.axis_index("row"), lax.axis_index("col")
    chip, core = row // 2, lax.rem(row, 2)
    sibling = (row + 1 - 2 * core, col)
    row_up, row_down = lax.rem(row + 1, rows), lax.rem(row + rows - 1, rows)
    col_up, col_down = lax.rem(col + 1, cols), lax.rem(col + cols - 1, cols)
    row_other = lax.rem(row + rows + 2 * core - 1, rows)

    def chip_at(offset):
        return lax.rem(chip + offset, chips)

    def col_at(offset):
        return lax.rem(col + offset, cols)

    def on_chip(q):
        return (2 * q + core, col)

    def push(src, dst, send, recv, device):
        return pltpu.make_async_remote_copy(
            src_ref=src, dst_ref=dst, send_sem=send, recv_sem=recv,
            device_id=device, device_id_type=MESH,
        )

    fetches = [
        pltpu.make_async_copy(src, dst, loads.at[n])
        for n, (src, dst) in enumerate(
            [(lie_hbm, lie_ref), (snap_hbm, snap_ref), (start_hbm, start_ref)]
        )
    ]
    for copy in fetches:
        copy.start()
    barrier = pltpu.get_barrier_semaphore()
    partners = [sibling, (row_other, col)]
    partners += [on_chip(chip_at(o)) for o in range(1, chips)]
    partners += [(row, col_at(o)) for o in range(1, cols)]
    for device in partners:
        pl.semaphore_signal(barrier, inc=1, device_id=device, device_id_type=MESH)

    comps, rank = sk_ref.shape[0], sk_ref.shape[-1]
    fetches[0].wait()
    sk_cols[...] = lie_ref[...].reshape(-1, rank).T.reshape(sk_cols.shape)
    fetches[1].wait()
    snaps = snap_ref[...].reshape(-1, snap_ref.shape[-1])

    waves = range(sc1.shape[0])

    def projection(which):
        half = jnp.dot(sk_cols[which], snaps, preferred_element_type=F32)
        size = sc1.shape[-1]
        return [half[:, w * size:(w + 1) * size].reshape(sc1.shape[1:]) for w in waves]

    for w, value in enumerate(projection(1 - core)):
        sc1[w] = value
    pl.semaphore_wait(barrier, len(partners))
    a1 = [push(sc1.at[w], rc1.at[w], a1s.at[w], a1r.at[w], sibling) for w in waves]
    for copy in a1:
        copy.start()
    mine = projection(core)
    for c in range(comps):
        sk_ref[c] = lie_ref[:, c].reshape(sk_ref.shape[1:])
    nx, plane = sk_ref.shape[1:3]
    halos = [
        push(sk_ref.at[:, nx - 1], hx.at[0], hs.at[0], hr.at[0], (row_up, col)),
        push(sk_ref.at[:, 0], hx.at[1], hs.at[1], hr.at[1], (row_down, col)),
        push(sk_ref.at[:, :, pl.ds(plane - 16, 16)], hy.at[0], hs.at[2], hr.at[2], (row, col_up)),
        push(sk_ref.at[:, :, pl.ds(0, 16)], hy.at[1], hs.at[3], hr.at[3], (row, col_down)),
    ]
    a2 = []
    for w in waves:
        a1[w].wait_recv()
        acc1[w] = mine[w] + rc1[w]
        for o in range(1, chips):
            q = chip_at(o)
            copy = push(
                acc1.at[w, q], rc2.at[w, chip],
                a2s.at[w * chips + o], a2r.at[w * chips + chip], on_chip(q),
            )
            copy.start()
            a2.append(copy)
    for copy in halos:
        copy.start()

    extent = diff.shape[0]
    cells = nx * plane
    place = lax.broadcasted_iota(jnp.int32, (extent, cells), 0)
    for d, (fore, aft) in enumerate(zip(*neighbour_columns(nx, plane // span, span))):
        diff[:, d * cells:(d + 1) * cells] = (
            jnp.where(place == fore, 0.5, 0.0) - jnp.where(place == aft, 0.5, 0.0)
        ).astype(BF16)

    a3 = []
    for w in waves:
        total = acc1[w, chip]
        for o in range(1, chips):
            q = chip_at(o)
            block = rc2.at[w, q]
            push(block, block, a2s.at[0], a2r.at[w * chips + q], sibling).wait_recv()
            total = total + rc2[w, q]
        rc3[w, col] = total
        own = rc3.at[w, col]
        for o in range(1, cols):
            copy = push(
                own, own, a3s.at[w * cols + o], a3r.at[w * cols + col], (row, col_at(o))
            )
            copy.start()
            a3.append(copy)
    a4, a5 = [], []
    for w in waves:
        for o in range(1, cols):
            z = col_at(o)
            block = rc3.at[w, z]
            push(block, block, a3s.at[0], a3r.at[w * cols + z], sibling).wait_recv()
        total = rc3[w, 0]
        for z in range(1, cols):
            total = total + rc3[w, z]
        cfull[w, core, chip] = total
        own = cfull.at[w, core, chip]
        for o in range(1, chips):
            copy = push(
                own, own, a4s.at[w * chips + o], a4r.at[w * chips + chip], on_chip(chip_at(o))
            )
            copy.start()
            a4.append(copy)
        copy = push(own, own, a5s.at[w * chips], a5r.at[w * chips + chip], sibling)
        copy.start()
        a5.append(copy)
    for w in waves:
        for o in range(1, chips):
            q = chip_at(o)
            block = cfull.at[w, core, q]
            push(block, block, a4s.at[0], a4r.at[w * chips + q], sibling).wait_recv()
            copy = push(block, block, a5s.at[w * chips + o], a5r.at[w * chips + q], sibling)
            copy.start()
            a5.append(copy)
    for w in waves:
        for q in range(chips):
            block = cfull.at[w, 1 - core, q]
            push(block, block, a5s.at[0], a5r.at[w * chips + q], sibling).wait_recv()

    coeffs = jnp.concatenate([cfull[w].reshape(rank, -1) for w in waves], axis=1)
    fetches[2].wait()
    start = start_ref[...]
    modes, rank = start.shape
    coeffs_h, coeffs_l = halves(coeffs)
    projected = jnp.dot(
        wide_left(start),
        jnp.concatenate([coeffs_h, coeffs_l, coeffs_h], axis=0),
        preferred_element_type=F32,
    )
    y_matrix = lax.dot_general(
        wide_left(projected),
        jnp.concatenate([coeffs_h, coeffs_l, coeffs_h], axis=1),
        NT, preferred_element_type=F32,
    )
    polar = y_matrix / jnp.sqrt(jnp.sum(y_matrix * y_matrix) + 1e-06)
    polar = jnp.concatenate([polar, jnp.zeros((-modes % 128, rank), F32)], axis=0)
    for _ in range(ITERS):
        high, low = halves(polar)
        gram = lax.dot_general(
            jnp.concatenate([high, high, low], axis=1),
            jnp.concatenate([high, low, high], axis=1),
            NT, preferred_element_type=F32,
        )
        polar = 1.5 * polar - 0.5 * jnp.dot(
            wide_left(gram),
            jnp.concatenate([high, low, high], axis=0),
            preferred_element_type=F32,
        )
    polar = polar[:modes]
    basis = polar.astype(BF16)

    for copy in halos:
        copy.wait_recv()
    for c in range(3):
        inner = sk_ref[c].reshape(cells, rank)
        outer = jnp.concatenate(
            [hx[0, c], hx[1, c], hy[0, c].reshape(-1, rank), hy[1, c].reshape(-1, rank)], axis=0
        )
        field = lax.dot_general(basis, inner, NT, preferred_element_type=F32).astype(BF16)
        rim = lax.dot_general(basis, outer, NT, preferred_element_type=F32).astype(BF16)
        phi[c] = field.astype(F32).reshape(phi.shape[1:])
        phi_all[c * cells:(c + 1) * cells] = lax.dot_general(
            inner, basis, NT, preferred_element_type=F32
        ).astype(BF16)
        slopes = jnp.dot(
            jnp.concatenate([field, rim], axis=1), diff[...], preferred_element_type=F32
        ).astype(BF16)
        for d in range(3):
            grad[d, c] = slopes[:, d * cells:(d + 1) * cells]

    blocks = gfull.shape[2]
    count = 128 * blocks // modes

    def part(which, q):
        group_at = which * chips + q
        for ct in range(cells // 128):
            lanes = slice(ct * 128, ct * 128 + 128)
            for group in range(0, count, 4):
                some = range(group, min(group + 4, count))
                p = [
                    [
                        jnp.broadcast_to(phi[d, group_at, i:i + 1, lanes], (16, 128)).astype(BF16)
                        for d in range(3)
                    ]
                    for i in some
                ]
                for c in range(3):
                    for jt in range(0, modes, 16):
                        g = [grad[d, c, jt:jt + 16, lanes] for d in range(3)]
                        for i, pi in zip(some, p):
                            adv[
                                i * modes + jt:i * modes + jt + 16,
                                c * cells + ct * 128:c * cells + ct * 128 + 128,
                            ] = pi[0] * g[0] + pi[1] * g[1] + pi[2] * g[2]
        value = jnp.dot(adv[...], phi_all[...], preferred_element_type=F32)
        return [value[n * 128:n * 128 + 128].T for n in range(blocks)]

    def theirs(step, carry):
        q = chip_at(step + 1)
        for n, value in enumerate(part(1 - core, q)):
            sg1[q, n] = value.astype(BF16)
        push(sg1.at[q], rg1.at[q], g1s.at[q], g1r.at[q], sibling).start()
        return carry

    lax.fori_loop(0, chips, theirs, 0)

    def ours(q):
        values = part(core, q)
        push(rg1.at[q], rg1.at[q], g1s.at[q], g1r.at[q], sibling).wait_recv()
        return [value + rg1[q, n].astype(F32) for n, value in enumerate(values)]

    def for_others(step, carry):
        q = chip_at(step + 1)
        for n, value in enumerate(ours(q)):
            sg2[q, n] = value.astype(BF16)
        push(sg2.at[q], rg2.at[chip], g2s.at[q], g2r.at[chip], on_chip(q)).start()
        return carry

    lax.fori_loop(0, chips - 1, for_others, 0)
    sums = ours(chip)
    for o in range(1, chips):
        q = chip_at(o)
        push(rg2.at[q], rg2.at[q], g2s.at[q], g2r.at[q], sibling).wait_recv()
        sums = [value + rg2[q, n].astype(F32) for n, value in enumerate(sums)]

    share = blocks // cols
    later = []
    if share:
        for n, value in enumerate(sums):
            sg3[n // share, n % share] = value.astype(BF16)
        for o in range(1, cols):
            z = col_at(o)
            copy = push(sg3.at[z], rg3.at[col], g3s.at[z], g3r.at[col], (row, z))
            copy.start()
            later.append(copy)
        final = sg3[col].astype(F32)
        for o in range(1, cols):
            z = col_at(o)
            push(rg3.at[z], rg3.at[z], g3s.at[z], g3r.at[z], sibling).wait_recv()
            final = final + rg3[z].astype(F32)
        gfull[core, chip, pl.ds(col * share, share)] = final.astype(BF16)
        own = gfull.at[core, chip, pl.ds(col * share, share)]
        for o in range(1, cols):
            z = col_at(o)
            copy = push(own, own, g4s.at[z], g4r.at[col], (row, z))
            copy.start()
            later.append(copy)
    else:
        for n, value in enumerate(sums):
            rg3[col, n] = value.astype(BF16)
        for o in range(1, cols):
            z = col_at(o)
            copy = push(rg3.at[col], rg3.at[col], g3s.at[z], g3r.at[col], (row, z))
            copy.start()
            later.append(copy)
        for o in range(1, cols):
            z = col_at(o)
            push(rg3.at[z], rg3.at[z], g3s.at[z], g3r.at[z], sibling).wait_recv()
        final = rg3[0].astype(F32)
        for z in range(1, cols):
            final = final + rg3[z].astype(F32)
        gfull[core, chip] = final.astype(BF16)

    pieces = cols if share else 1
    width = blocks // pieces

    def piece(which, q, z):
        return gfull.at[which, q, pl.ds(z * width, width)]

    outs = []

    def write(which, q, z):
        for n in range(width):
            block = z * width + n
            slot = (which * chips + q) * blocks + block
            lanes = pl.ds(pl.multiple_of(slot * 128, 128), 128)
            copy = pltpu.make_async_copy(
                gfull.at[which, q, block], out_ref.at[:, lanes], stores.at[slot]
            )
            copy.start()
            outs.append(copy)

    def forward(q, z):
        part_of = piece(core, q, z)
        copy = push(part_of, part_of, g6s.at[q * pieces + z], g6r.at[q * pieces + z], sibling)
        copy.start()
        later.append(copy)
        write(core, q, z)

    order = [col_at(o) for o in range(pieces)] if share else [0]
    for o, z in enumerate(order):
        own = piece(core, chip, z)
        if o:
            push(own, own, g4s.at[z], g4r.at[z], sibling).wait_recv()
        for offset in range(1, chips):
            q = chip_at(offset)
            copy = push(
                own, own, g5s.at[q * pieces + z], g5r.at[chip * pieces + z], on_chip(q)
            )
            copy.start()
            later.append(copy)
        forward(chip, z)
    for z in order:
        for offset in range(1, chips):
            q = chip_at(offset)
            block = piece(core, q, z)
            slot = q * pieces + z
            push(block, block, g5s.at[slot], g5r.at[slot], sibling).wait_recv()
            forward(q, z)
    for z in order:
        for offset in range(chips):
            q = chip_at(offset)
            block = piece(1 - core, q, z)
            slot = q * pieces + z
            push(block, block, g6s.at[slot], g6r.at[slot], sibling).wait_recv()
            write(1 - core, q, z)

    for copy in outs:
        copy.wait()
    for copy in [*a1, *halos, *a2, *a3, *a4, *a5, *later]:
        copy.wait_send()
    for q in range(chips):
        push(sg1.at[q], rg1.at[q], g1s.at[q], g1r.at[q], sibling).wait_send()
    for o in range(1, chips):
        q = chip_at(o)
        push(sg2.at[q], rg2.at[q], g2s.at[q], g2r.at[q], sibling).wait_send()


def body(chips, cols, sketch, snapshots, start_block):
    nx, ny, nz, comps, rank = sketch.shape
    snaps = snapshots.shape[-1]
    modes = start_block.shape[1]
    cells = nx * ny * nz
    depth = rank // (2 * chips)
    lie = sketch.transpose(0, 1, 3, 2, 4).reshape(nx * ny, comps, nz, rank)
    snap = snapshots.transpose(0, 1, 3, 2, 4).reshape(nx * ny * comps, nz, snaps)
    extent = cells + 2 * ny * nz + 2 * nx * 16
    blocks = modes * modes // (2 * chips * 128)
    share = max(blocks // cols, 1)
    scale = 1.0 / math.sqrt(cells * 2 * chips * cols)
    waves = 2
    counts = [4, 4, waves, waves] + [waves * chips] * 2 + [waves * cols] * 2
    counts += [waves * chips] * 4
    pieces = cols if blocks // cols else 1
    counts += [chips] * 4 + [cols] * 4 + [chips * pieces] * 4
    tensor = pl.pallas_call(
        functools.partial(kernel, chips, cols, nz),
        out_shape=jax.ShapeDtypeStruct((modes, modes * modes), BF16),
        in_specs=[pl.BlockSpec(memory_space=pltpu.HBM)] * 3,
        out_specs=pl.BlockSpec(memory_space=pltpu.HBM),
        scratch_shapes=[
            pltpu.VMEM(lie.shape, BF16),
            pltpu.VMEM(snap.shape, BF16),
            pltpu.VMEM((modes, rank), F32),
            pltpu.SemaphoreType.DMA((3,)),
            pltpu.SemaphoreType.DMA((2 * chips * blocks,)),
            pltpu.VMEM((comps, nx, ny * nz, rank), BF16),
            pltpu.VMEM((2, rank // 2, comps * cells), BF16),
            pltpu.VMEM((2, comps, ny * nz, rank), BF16),
            pltpu.VMEM((2, comps, nx, 16, rank), BF16),
            pltpu.VMEM((waves, chips, depth, snaps // waves), F32),
            pltpu.VMEM((waves, chips, depth, snaps // waves), F32),
            pltpu.VMEM((waves, chips, depth, snaps // waves), F32),
            pltpu.VMEM((waves, chips, depth, snaps // waves), F32),
            pltpu.VMEM((waves, cols, depth, snaps // waves), F32),
            pltpu.VMEM((waves, 2, chips, depth, snaps // waves), F32),
            pltpu.VMEM((extent, 3 * cells), BF16),
            pltpu.VMEM((comps, 2 * chips, modes // (2 * chips), cells), F32),
            pltpu.VMEM((comps * cells, modes), BF16),
            pltpu.VMEM((3, comps, modes, cells), BF16),
            pltpu.VMEM((blocks * 128, comps * cells), BF16),
            pltpu.VMEM((chips, blocks, modes, 128), BF16),
            pltpu.VMEM((chips, blocks, modes, 128), BF16),
            pltpu.VMEM((chips, blocks, modes, 128), BF16),
            pltpu.VMEM((chips, blocks, modes, 128), BF16),
            pltpu.VMEM((cols, share, modes, 128), BF16),
            pltpu.VMEM((cols, share, modes, 128), BF16),
            pltpu.VMEM((2, chips, blocks, modes, 128), BF16),
        ] + [pltpu.SemaphoreType.DMA((n,)) for n in counts],
        compiler_params=pltpu.CompilerParams(
            collective_id=0, has_side_effects=True, vmem_limit_bytes=60 * 1024 * 1024
        ),
    )(lie, snap, start_block.T)
    return tensor.astype(F32) * scale


def solution(mesh):
    chips, cols = mesh.shape["row"] // 2, mesh.shape["col"]
    return jax.shard_map(
        functools.partial(body, chips, cols),
        mesh=mesh,
        in_specs=(P("row", "col", None, None, None), P("row", "col", None, None, None), P()),
        out_specs=P(),
        check_vma=False,
    )
```
